128 devices in a mesh: tile: 32 (over z, y, core), col: 4 (over x).
Axes of the slice: x: 4, y: 4, z: 4, core: 2. Of those that a mesh axis runs over, the one named last changes fastest.
Arguments:
- spectrum: float32 [2, 2048, 2048], P(None, 'tile', 'col'), may hold values from -6 to 6
- pupil_field: float32 [2, 512, 512], replicated, may hold values from -4 to 4
- amplitude: float32 [512, 512, 512], P(('tile', 'col')), may hold values from 0 to 2
- offsets: int32 [512, 2], P(('tile', 'col')), may hold values from 0 to 24, as said below
Outputs:
- updated: float32 [2, 2048, 2048], P(None, 'tile', 'col')
The draws below stay inside these ranges and needn't reach their ends.
Inputs may be any that keep to these rules, and one draw needn't show every extreme that they name: `offsets`: row l gives LED l's window in blocks of 64 by 64 cells: column 0 is its first block row, column 1 its first block column; a window spans 8 blocks each way and lies inside the spectrum. LED l belongs to the device at position l // 4 in the order of the images. The first block rows of one device's LEDs are distinct multiples of 8, so that its windows together cover every block row once.
All inputs are finite; a program needn't handle non-finite values.
Results may differ from the reference program's by a relative error of at most 0.0035.
Values may be sent and summed in bfloat16 or wider, within the bound.
No kernel may reach another device: no remote copies, remote signals or barrier semaphores. Data moves between devices by JAX's collectives and lax.ppermute only.
A program may use at most 192 MiB of HBM per device.

```python
import jax
import jax.numpy as jnp
from jax import lax

WIN = 512
BH = 64
WB = 8
LED_DEV = 4
NR = 2048
NC = 2048
LEDS = 512


def draw_offsets(key, part):
    key = jax.random.fold_in(key, 11)
    subkeys = jax.random.split(key, 6)
    device_count = LEDS // LED_DEV
    col_blocks = NC // BH
    half_cols = (col_blocks - WB) // 2
    perm_keys = jax.random.split(subkeys[0], device_count)
    orders = jax.vmap(lambda one_key: jax.random.permutation(one_key, LED_DEV))(perm_keys).astype(jnp.int32)
    led_pos = jnp.arange(LED_DEV, dtype=jnp.int32)[None, :]
    device_ids = jnp.arange(device_count, dtype=jnp.int32)[:, None]
    row_starts = orders * WB
    col_starts = jax.random.randint(subkeys[2], (device_count, LED_DEV), 0, half_cols + 1) + jax.random.randint(subkeys[3], (device_count, LED_DEV), 0, col_blocks - WB - half_cols + 1)
    top_device = jax.random.randint(subkeys[4], (), 0, device_count)
    low_device = (top_device + 1 + jax.random.randint(subkeys[5], (), 0, device_count - 1)) % device_count
    col_starts = jnp.where((device_ids == top_device) & (led_pos == 0), col_blocks - WB, col_starts)
    col_starts = jnp.where((device_ids == low_device) & (led_pos == 0), 0, col_starts)
    return jnp.stack([row_starts, col_starts], axis=-1).reshape(LEDS, 2).astype(jnp.int32)


def level_of(rng, dims, cuts, low, high):
    gain, own = 1.0, jax.random.fold_in(rng, 6)
    for axis_at, parts in cuts:
        heights = jnp.exp(jax.random.uniform(jax.random.fold_in(own, axis_at), (parts,), jnp.float32, low / len(cuts), high / len(cuts)))
        gain = gain * jnp.repeat(heights, dims[axis_at] // parts).reshape([-1 if axis == axis_at else 1 for axis in range(len(dims))])
    return gain


def bell_draw(rng, extent, deviation, limit, shards=(), held_as=jnp.bfloat16):
    entries = deviation * jax.random.normal(rng, extent, jnp.float32)
    if shards:
        entries = entries * level_of(rng, extent, shards, -0.22, 0.18)
    return jnp.clip(entries, -limit, limit).astype(held_as)


def setup_inputs(seed: int = 0) -> dict:
    key_list = jax.random.split(jax.random.key(seed), 5)
    return {
        "spectrum": bell_draw(key_list[0], (2, NR, NC), 1.0, 6.0, ((1, 32), (2, 4)), jnp.float32),
        "pupil_field": bell_draw(key_list[1], (2, WIN, WIN), 0.7, 4.0, (), jnp.float32),
        "amplitude": jnp.clip(2.0 * jax.random.uniform(key_list[2], (LEDS, WIN, WIN), jnp.float32) ** level_of(key_list[2], (LEDS, WIN, WIN), ((0, 128),), -0.2, 0.2), 0.0, 2.0),
        "offsets": draw_offsets(jax.random.fold_in(key_list[4], 71), 0),
    }


floor_sq = 0.25
step_size = 0.5

def reference(spectrum, pupil_field, amplitude, offsets):
    lowered = spectrum.astype(jnp.bfloat16)
    pupil_re = pupil_field[0]
    pupil_im = pupil_field[1]
    grad_total = jnp.zeros(spectrum.shape, jnp.float32)

    def one_led(grad_sum, inputs):
        measured, placement = inputs
        zero_index = jnp.zeros((), jnp.int32)
        row_start = (placement[0] * BH).astype(jnp.int32)
        col_start = (placement[1] * BH).astype(jnp.int32)
        window = lax.dynamic_slice(lowered, (zero_index, row_start, col_start), (2, WIN, WIN)).astype(jnp.float32)
        exit_re = pupil_re * window[0] - pupil_im * window[1]
        exit_im = pupil_re * window[1] + pupil_im * window[0]
        exit_field = jnp.fft.ifft2(lax.complex(exit_re, exit_im), norm='ortho')
        field_re = jnp.real(exit_field)
        field_im = jnp.imag(exit_field)
        factor = 1.0 - measured / jnp.sqrt(field_re * field_re + field_im * field_im + floor_sq)
        spectral = jnp.fft.fft2(lax.complex(field_re * factor, field_im * factor), norm='ortho')
        spec_re = jnp.real(spectral)
        spec_im = jnp.imag(spectral)
        update_re = pupil_re * spec_re + pupil_im * spec_im
        update_im = pupil_re * spec_im - pupil_im * spec_re
        rounded = lax.optimization_barrier(jnp.stack([update_re, update_im]).astype(jnp.bfloat16))
        update = rounded.astype(jnp.float32)
        current = lax.dynamic_slice(grad_sum, (zero_index, row_start, col_start), (2, WIN, WIN))
        grad_sum = lax.dynamic_update_slice(grad_sum, current + update, (zero_index, row_start, col_start))
        return (grad_sum, None)
    grad_total = lax.scan(one_led, grad_total, (amplitude, offsets))[0]
    return spectrum - step_size * grad_total
```

```python
import math

import jax
import jax.numpy as jnp
import numpy as np
from jax import lax
from jax.experimental import pallas as pl
from jax.experimental.pallas import tpu as pltpu
from jax.sharding import PartitionSpec as P

floor_sq = 0.25
step_size = 0.5
LANES = 128
DEPTHS, HEIGHTS, CORES = 4, 4, 2
TILE = 256
DEPTH, HEIGHT, CORE, COLUMN, NEAR = range(5)
VMEM = pl.BlockSpec(memory_space=pltpu.VMEM)
SMEM = pl.BlockSpec(memory_space=pltpu.SMEM)


def params(mib, **more):
    return pltpu.CompilerParams(vmem_limit_bytes=mib * 2**20, **more)


def split_table(table):
    high = table.astype(jnp.bfloat16)
    low = (table - high.astype(np.float64)).astype(jnp.bfloat16)
    return np.stack([high, low])


def dft_tables(length, block):
    counter = np.arange(length)
    angles = (counter[:, None] * counter[None, :] % length) * (2.0 * math.pi / length)
    cosine = np.cos(angles) / math.sqrt(length)
    sine = np.sin(angles) / math.sqrt(length)
    half = length // 2
    even_cos, even_sin = cosine[::2, :half], sine[::2, :half]
    rows = np.block([[even_cos, -even_sin], [even_sin, even_cos]])
    right = np.block([[cosine, sine], [-sine, cosine]])
    blocks = length // block
    order = np.arange(2 * length).reshape(2, blocks, block).transpose(1, 0, 2).reshape(-1)
    turn = np.arange(half)[:, None] * (2.0 * math.pi / length) * np.ones((1, LANES))
    turn = np.stack([np.cos(turn), np.sin(turn)]).astype(np.float32)
    return split_table(rows), split_table(right[order]), split_table(right[:, order]), turn


def swap_halves(packed):
    return pltpu.roll(packed, LANES // 2, axis=packed.ndim - 1)


def pack_pair(first, second, low_half):
    left = jnp.where(low_half, first, swap_halves(second))
    right = jnp.where(low_half, swap_halves(first), second)
    return left, right


def low_lanes(rows):
    return lax.broadcasted_iota(jnp.int32, (rows, LANES), 1) < LANES // 2


def prep_kernel(place_ref, spectrum_ref, keep_ref, send_ref, pair_ref):
    rows, width = spectrum_ref.shape[1:]
    low_half = low_lanes(rows // 2)
    first_core = place_ref[CORE] == 0
    for group in range(width // LANES):
        pair_ref[group] = spectrum_ref[:, :, pl.ds(group * LANES, LANES)]
        halves = []
        for half in range(2):
            chosen = pl.ds(half, rows // 2, stride=2)
            real = pair_ref[group, 0, chosen].astype(jnp.bfloat16).astype(jnp.float32)
            imag = pair_ref[group, 1, chosen].astype(jnp.bfloat16).astype(jnp.float32)
            halves.append(pack_pair(real, imag, low_half))
        for side in range(2):
            even, odd = halves[0][side], halves[1][side]
            block = 2 * group + side
            keep_ref[block] = jnp.where(first_core, even, odd).astype(jnp.bfloat16)
            send_ref[block] = jnp.where(first_core, odd, even).astype(jnp.bfloat16)


def join_kernel(place_ref, own_ref, other_ref, out_ref):
    core = place_ref[CORE]
    out_ref[core] = own_ref[...]
    out_ref[1 - core] = other_ref[...]


def pupil_kernel(pupil_ref, same_ref, cross_ref, pair_ref):
    bands, _, rows = same_ref.shape[1:4]
    low_half = low_lanes(rows)

    @pl.loop(0, bands)
    def _(band):
        for group in range(pupil_ref.shape[2] // LANES):
            pair_ref[group] = pupil_ref[:, pl.ds(band * 2 * rows, 2 * rows), pl.ds(group * LANES, LANES)]
            for half in range(2):
                chosen = pl.ds(half, rows, stride=2)
                real = pair_ref[group, 0, chosen]
                imag = pair_ref[group, 1, chosen]
                left, right = pack_pair(real, real, low_half)
                same_ref[half, band, 2 * group] = left
                same_ref[half, band, 2 * group + 1] = right
                left, right = pack_pair(-imag, imag, low_half)
                cross_ref[half, band, 2 * group] = left
                cross_ref[half, band, 2 * group + 1] = right


def select_kernel(place_ref, starts_ref, *refs):
    near, outs, rows_ref = refs[:4], refs[4:12], refs[12]
    blocks = near[0].shape[2]
    for source in range(4):
        first = CORES * lax.rem(place_ref[NEAR] + 4 - source, 4)
        for part in range(near[0].shape[0]):
            rows_ref[pl.ds(first, CORES), pl.ds(part * blocks, blocks)] = near[source][part]
    span = outs[0].shape[1]
    for peer in range(len(outs)):
        for row in range(rows_ref.shape[0]):
            outs[peer][row] = rows_ref[row, pl.ds(starts_ref[peer, row], span)]


def table_dot(left, right):
    return jnp.dot(left, right, preferred_element_type=jnp.float32)


def led_kernel(place_ref, leds_ref, *refs):
    incoming, outgoing = refs[:8], refs[15:23]
    measured_ref, same_ref, cross_ref, rows_ref, spread_ref, gather_ref, turn_ref = refs[8:15]
    held_ref, packed_ref, stacked_ref = refs[23:]
    depth, height = place_ref[DEPTH], place_ref[HEIGHT]
    first_core = place_ref[CORE] == 0
    steps = held_ref.shape[0]
    bands, blocks, rows = held_ref.shape[2:5]
    half_size = bands * rows
    size = 2 * half_size

    for step in range(steps):
        source = (steps - step) % steps
        held_ref[step, 0] = jnp.where(
            first_core, incoming[2 * source][...], incoming[2 * source + 1][...]
        )
        taken = pl.ds(CORES * lax.rem(depth + step, steps), CORES)
        for source in range(HEIGHTS):
            kept = pl.ds(CORES * lax.rem(height + HEIGHTS - source, HEIGHTS), CORES)
            held_ref[step, 1, kept] = jnp.where(
                first_core, incoming[2 * source + 1][taken], incoming[2 * source][taken]
            )

    turn_re = jnp.concatenate([turn_ref[0]] * (TILE // LANES), axis=1)
    turn_im = jnp.concatenate([turn_ref[1]] * (TILE // LANES), axis=1)

    def row_transform(half, lanes):
        moved = table_dot(rows_ref[0], stacked_ref[half, :, lanes])
        moved += table_dot(rows_ref[1], stacked_ref[half, :, lanes])
        return moved[:half_size], moved[half_size:]

    @pl.loop(0, steps)
    def _(step):
        led = leds_ref[step]

        @pl.loop(0, bands)
        def _(band):
            for half in range(2):
                for block in range(blocks):
                    window = held_ref[step, half, band, block].astype(jnp.float32)
                    wave = same_ref[half, band, block] * window
                    wave += cross_ref[half, band, block] * swap_halves(window)
                    packed_ref[
                        pl.ds(half * half_size + band * rows, rows), pl.ds(block * LANES, LANES)
                    ] = wave.astype(jnp.bfloat16)

        for part in range(2):
            for tile in range(size // TILE):
                lanes = pl.ds(part * size + tile * TILE, TILE)
                product = table_dot(packed_ref[...], spread_ref[0, :, lanes])
                product += table_dot(packed_ref[...], spread_ref[1, :, lanes])
                product = product.astype(jnp.bfloat16)
                for half in range(2):
                    stacked_ref[
                        half, pl.ds(part * half_size, half_size), pl.ds(tile * TILE, TILE)
                    ] = product[half * half_size:(half + 1) * half_size]

        for tile in range(size // TILE):
            lanes = pl.ds(tile * TILE, TILE)
            even_re, even_im = row_transform(0, lanes)
            odd_re, odd_im = row_transform(1, lanes)
            turned_re = odd_re * turn_re - odd_im * turn_im
            turned_im = odd_re * turn_im + odd_im * turn_re

            def residual(real, imag, start):
                measured = measured_ref[led, pl.ds(start, half_size), lanes]
                factor = 1.0 - measured * lax.rsqrt(real * real + imag * imag + floor_sq)
                return real * factor, -imag * factor

            top_re, top_im = residual(even_re + turned_re, even_im + turned_im, 0)
            low_re, low_im = residual(even_re - turned_re, even_im - turned_im, half_size)
            stacked_ref[0, :half_size, lanes] = (top_re + low_re).astype(jnp.bfloat16)
            stacked_ref[0, half_size:, lanes] = (top_im + low_im).astype(jnp.bfloat16)
            gap_re, gap_im = top_re - low_re, top_im - low_im
            stacked_ref[1, :half_size, lanes] = (gap_re * turn_re - gap_im * turn_im).astype(
                jnp.bfloat16
            )
            stacked_ref[1, half_size:, lanes] = (gap_re * turn_im + gap_im * turn_re).astype(
                jnp.bfloat16
            )
            for half in range(2):
                real, imag = row_transform(half, lanes)
                kept = pl.ds(half * half_size, half_size)
                packed_ref[kept, lanes] = real.astype(jnp.bfloat16)
                packed_ref[kept, pl.ds(size + tile * TILE, TILE)] = imag.astype(jnp.bfloat16)

        for tile in range(2 * size // TILE):
            lanes = pl.ds(tile * TILE, TILE)
            product = table_dot(packed_ref[...], gather_ref[0, :, lanes])
            product += table_dot(packed_ref[...], gather_ref[1, :, lanes])
            for part in range(TILE // LANES):
                block = tile * (TILE // LANES) + part
                for half in range(2):
                    for band in range(bands):
                        start = half * half_size + band * rows
                        spectral = product[start:start + rows, part * LANES:(part + 1) * LANES]
                        update = same_ref[half, band, block] * spectral
                        update += cross_ref[half, band, block] * swap_halves(spectral)
                        held_ref[step, half, band, block] = update.astype(jnp.bfloat16)

    for source in range(HEIGHTS):
        for side in range(CORES):
            even_rows = place_ref[CORE] == side
            kept = pl.ds(CORES * lax.rem(height + HEIGHTS - source, HEIGHTS), CORES)
            for step in range(steps):
                taken = pl.ds(CORES * lax.rem(depth + step, steps), CORES)
                outgoing[2 * source + side][taken] = jnp.where(
                    even_rows, held_ref[(steps - source) % steps, 0, taken], held_ref[step, 1, kept]
                )


def collect_kernel(place_ref, starts_ref, *refs):
    updates, outs, total_ref = refs[:8], refs[8:12], refs[12]
    span = updates[0].shape[1]
    for peer in range(4):
        first = CORES * lax.rem(place_ref[NEAR] + peer, 4)
        for side in range(CORES):
            total_ref[...] = jnp.zeros_like(total_ref)
            for source in range(8):
                place = pl.ds(starts_ref[source, first + side], span)
                total_ref[place] = total_ref[place] + updates[source][first + side].astype(jnp.float32)
            outs[peer][side] = total_ref[...].astype(outs[peer].dtype)


def columns_kernel(place_ref, *refs):
    parts, outs = refs[:4], refs[4:]
    blocks = outs[0].shape[1]
    for peer in range(len(outs)):
        place = pl.ds(lax.rem(place_ref[COLUMN] + peer, len(outs)) * blocks, blocks)
        for side in range(CORES):
            total = parts[0][side, place].astype(jnp.float32)
            for part in parts[1:]:
                total = total + part[side, place].astype(jnp.float32)
            outs[peer][side] = total.astype(outs[peer].dtype)


def halves_kernel(place_ref, part0_ref, part1_ref, part2_ref, part3_ref, keep_ref, send_ref):
    core = place_ref[CORE]
    for out_ref, side in ((keep_ref, core), (send_ref, 1 - core)):
        total = part0_ref[side].astype(jnp.float32)
        for part_ref in (part1_ref, part2_ref, part3_ref):
            total = total + part_ref[side].astype(jnp.float32)
        out_ref[...] = total


def final_kernel(place_ref, own_ref, other_ref, spectrum_ref, out_ref, pair_ref):
    rows, width = spectrum_ref.shape[1:]
    low_half = low_lanes(rows // 2)
    first_core = place_ref[CORE] == 0
    for group in range(width // LANES):
        for half in range(2):
            sums = []
            for block in (2 * group, 2 * group + 1):
                pair = (own_ref[block], other_ref[block])
                sums.append(jnp.where(first_core, pair[half], pair[1 - half]))
            real, imag = pack_pair(sums[0], sums[1], low_half)
            chosen = pl.ds(half, rows // 2, stride=2)
            pair_ref[group, 0, chosen] = -step_size * real
            pair_ref[group, 1, chosen] = step_size * imag
        lanes = pl.ds(group * LANES, LANES)
        out_ref[:, :, lanes] = spectrum_ref[:, :, lanes] + pair_ref[group]


def call(kernel, outs, inputs, mib, name, scalars=0, scratch=(), flops=0):
    size = sum(math.prod(out.shape) * out.dtype.itemsize for out in outs)
    size += sum(math.prod(array.shape) * array.dtype.itemsize for array in inputs)
    return pl.pallas_call(
        kernel,
        out_shape=tuple(outs),
        in_specs=[SMEM] * scalars + [VMEM] * (len(inputs) - scalars),
        out_specs=(VMEM,) * len(outs),
        scratch_shapes=list(scratch),
        compiler_params=params(mib),
        cost_estimate=pl.CostEstimate(flops=flops, bytes_accessed=size, transcendentals=0),
        name=name,
    )(*inputs)


TILES = DEPTHS * HEIGHTS * CORES


def tile_of(depth, height, core):
    return (depth % DEPTHS * HEIGHTS + height % HEIGHTS) * CORES + core


def tile_moves(even_move, odd_move):
    pairs = []
    for tile in range(TILES):
        depth, height, core = tile // (HEIGHTS * CORES), tile // CORES % HEIGHTS, tile % CORES
        pairs.append((tile, tile_of(*(odd_move if core else even_move)(depth, height))))
    return pairs


def far_moves(steps, side):
    return tile_moves(
        lambda depth, height: (depth + steps, height, side),
        lambda depth, height: (depth, height + steps, 1 - side),
    )


def near_moves(steps):
    return tile_moves(
        lambda depth, height: (depth, height + steps, 0),
        lambda depth, height: (depth + steps, height, 1),
    )


def reverse(moves):
    return [(target, source) for source, target in moves]


def send(array, moves, axis="tile"):
    return lax.ppermute(array, axis, moves)


def on_device(spectrum, pupil_field, amplitude, offsets):
    columns = lax.axis_size("col")
    tile, column = lax.axis_index("tile"), lax.axis_index("col")
    depth, height, core = tile // (HEIGHTS * CORES), tile // CORES % HEIGHTS, tile % CORES
    block_rows, own_width = spectrum.shape[1:]
    size = pupil_field.shape[1]
    span = size // block_rows
    own_blocks = own_width // block_rows
    band_blocks = own_blocks * columns
    rows = block_rows // 2
    bf16, f32 = jnp.bfloat16, jnp.float32
    shaped = lambda *shape, dtype=bf16: jax.ShapeDtypeStruct(shape, dtype)
    near = jnp.where(core == 0, height, depth)
    place = jnp.stack([depth, height, core, column, near]).astype(jnp.int32)
    swap = [(t, t ^ 1) for t in range(TILES)]

    wanted = jnp.arange(DEPTHS, dtype=jnp.int32) * span
    mine = offsets[None, :, 0] == wanted[:, None]
    slots = jnp.arange(offsets.shape[0], dtype=jnp.int32)[None]
    leds = jnp.roll(jnp.sum(jnp.where(mine, slots, 0), axis=1), -depth).astype(jnp.int32)
    firsts = jnp.sum(jnp.where(mine, offsets[None, :, 1], 0), axis=1).astype(jnp.int32)
    chip = jnp.stack([firsts, send(firsts, swap)])
    chips = jnp.stack([chip] + [send(chip, reverse(far_moves(steps, 0))) for steps in range(1, 4)])
    by_row = jnp.repeat(chips, CORES, axis=2)
    same_band = jnp.broadcast_to(lax.dynamic_slice_in_dim(chips, depth, 1, 2), by_row.shape)
    starts = jnp.where(core == 0, same_band, by_row).reshape(8, span).astype(jnp.int32)

    pairs = lambda width: [pltpu.VMEM((width // LANES, 2, block_rows, LANES), f32)]
    part_shape = (own_blocks, rows, LANES)
    keep, give = call(
        prep_kernel,
        [shaped(*part_shape)] * 2,
        [place, spectrum],
        16,
        "prep",
        scalars=1,
        scratch=pairs(own_width),
    )
    joined, = call(
        join_kernel, [shaped(CORES, *part_shape)], [place, keep, send(give, swap)], 16, "join", scalars=1
    )
    band = lax.all_gather(joined, "col", axis=0)
    near_parts = [band] + [send(band, near_moves(steps)) for steps in range(1, 4)]
    windows = call(
        select_kernel,
        [shaped(span, span, rows, LANES)] * 8,
        [place, starts] + near_parts,
        24,
        "select",
        scalars=2,
        scratch=[pltpu.VMEM((span, band_blocks, rows, LANES), bf16)],
    )
    far = [far_moves(steps, side) for steps in range(4) for side in range(CORES)]
    incoming = [windows[0]] + [send(windows[peer], far[peer]) for peer in range(1, 8)]

    pupil_shape = shaped(2, span, span, rows, LANES, dtype=f32)
    same, cross = call(pupil_kernel, [pupil_shape] * 2, [pupil_field], 32, "pupil", scratch=pairs(size))
    tables = [jnp.asarray(table) for table in dft_tables(size, block_rows)]
    updates = call(
        led_kernel,
        [shaped(span, span, rows, LANES)] * 8,
        [place, leds] + incoming + [amplitude, same, cross, *tables],
        48,
        "leds",
        scalars=2,
        scratch=[
            pltpu.VMEM((DEPTHS, 2, span, span, rows, LANES), bf16),
            pltpu.VMEM((size, 2 * size), bf16),
            pltpu.VMEM((2, size, size), bf16),
        ],
        flops=96 * size**3,
    )
    returned = [updates[0]] + [send(updates[peer], reverse(far[peer])) for peer in range(1, 8)]

    sum_shape = (CORES, band_blocks, rows, LANES)
    sums = call(
        collect_kernel,
        [shaped(*sum_shape, dtype=f32)] + [shaped(*sum_shape)] * 3,
        [place, starts] + returned,
        32,
        "collect",
        scalars=2,
        scratch=[pltpu.VMEM(sum_shape[1:], f32)],
    )
    near_sums = [sums[0]] + [send(sums[steps], near_moves(steps)) for steps in range(1, 4)]
    cut = call(
        columns_kernel,
        [shaped(CORES, *part_shape, dtype=f32)] + [shaped(CORES, *part_shape)] * (columns - 1),
        [place] + near_sums,
        24,
        "columns",
        scalars=1,
    )
    along = lambda steps: [(c, (c + steps) % columns) for c in range(columns)]
    parts = [cut[0]] + [send(cut[steps], along(steps), "col") for steps in range(1, columns)]
    keep, give = call(
        halves_kernel, [shaped(*part_shape, dtype=f32)] * 2, [place] + parts, 16, "halves", scalars=1
    )
    return call(
        final_kernel,
        [shaped(*spectrum.shape, dtype=f32)],
        [place, keep, send(give, swap), spectrum],
        16,
        "final",
        scalars=1,
        scratch=pairs(own_width),
    )[0]


def solution(mesh):
    in_specs = (
        P(None, "tile", "col"),
        P(),
        P(("tile", "col"), None, None),
        P(("tile", "col"), None),
    )
    return jax.shard_map(
        on_device, mesh=mesh, in_specs=in_specs, out_specs=P(None, "tile", "col"), check_vma=False
    )
```

```python
import math

import jax
import jax.numpy as jnp
import numpy as np
from jax import lax
from jax.experimental import pallas as pl
from jax.experimental.pallas import tpu as pltpu
from jax.sharding import PartitionSpec as P

floor_sq = 0.25
step_size = 0.5
LANES = 128
DEPTHS, HEIGHTS, CORES = 4, 4, 2
TILE = 256
EARLY, LATE = (2, 0), (1, 3)
DEPTH, HEIGHT, CORE, COLUMN, NEAR = range(5)
VMEM = pl.BlockSpec(memory_space=pltpu.VMEM)
SMEM = pl.BlockSpec(memory_space=pltpu.SMEM)


def params(mib, **more):
    return pltpu.CompilerParams(vmem_limit_bytes=mib * 2**20, **more)


def split_table(table):
    high = table.astype(jnp.bfloat16)
    low = (table - high.astype(np.float64)).astype(jnp.bfloat16)
    return np.stack([high, low])


def dft_tables(length, block):
    half = length // 2
    counter = np.arange(half)
    angles = (counter[:, None] * counter[None, :] % half) * (2.0 * math.pi / half)
    cosine = np.cos(angles) / math.sqrt(length)
    sine = np.sin(angles) / math.sqrt(length)
    rows = np.block([[cosine, -sine], [sine, cosine]])
    right = np.block([[cosine, sine], [-sine, cosine]])
    pairs = length // (2 * block)
    lanes = np.arange(length).reshape(2, pairs, block).transpose(1, 0, 2).reshape(-1)
    turn = np.arange(half) * (2.0 * math.pi / length)
    turn = np.stack([np.cos(turn), np.sin(turn)])
    down = np.broadcast_to(turn[:, :, None], (2, half, LANES)).astype(np.float32)
    across = np.broadcast_to(turn[:, None, :], (2, 8, half)).astype(np.float32)
    tables = split_table(rows), split_table(right[lanes]), split_table(right[:, lanes])
    return *tables, down, across


def swap_halves(packed):
    return pltpu.roll(packed, LANES // 2, axis=packed.ndim - 1)


def pack_pair(first, second, low_half):
    left = jnp.where(low_half, first, swap_halves(second))
    right = jnp.where(low_half, swap_halves(first), second)
    return left, right


def lane_order(back=False):
    row = lax.broadcasted_iota(jnp.int32, (LANES, LANES), 0)
    column = lax.broadcasted_iota(jnp.int32, (LANES, LANES), 1)
    plain, moved = (column, row) if back else (row, column)
    block = LANES // 2
    inner = moved % block
    source = moved - inner + 2 * (inner % (block // 2)) + inner // (block // 2)
    return jnp.where(plain == source, 1.0, 0.0).astype(jnp.bfloat16)


def move_lanes(values, order):
    total = None
    for _ in range(3):
        part = values.astype(jnp.bfloat16)
        values = values - part.astype(jnp.float32)
        moved = jnp.dot(part, order, preferred_element_type=jnp.float32)
        total = moved if total is None else total + moved
    return total


def low_lanes(rows):
    return lax.broadcasted_iota(jnp.int32, (rows, LANES), 1) < LANES // 2


def prep_kernel(place_ref, spectrum_ref, keep_ref, send_ref, pair_ref):
    rows, width = spectrum_ref.shape[1:]
    low_half = low_lanes(rows // 2)
    first_core = place_ref[CORE] == 0
    order = lane_order()
    for group in range(width // LANES):
        for part in range(2):
            rounded = spectrum_ref[part, :, pl.ds(group * LANES, LANES)].astype(jnp.bfloat16)
            pair_ref[group, part] = jnp.dot(rounded, order, preferred_element_type=jnp.float32)
        halves = []
        for half in range(2):
            chosen = pl.ds(half, rows // 2, stride=2)
            halves.append(pack_pair(pair_ref[group, 0, chosen], pair_ref[group, 1, chosen], low_half))
        for side in range(2):
            even, odd = halves[0][side], halves[1][side]
            block = 2 * group + side
            keep_ref[block] = jnp.where(first_core, even, odd).astype(jnp.bfloat16)
            send_ref[block] = jnp.where(first_core, odd, even).astype(jnp.bfloat16)


def join_kernel(place_ref, own_ref, other_ref, out_ref):
    core = place_ref[CORE]
    out_ref[core] = own_ref[...]
    out_ref[1 - core] = other_ref[...]


def pupil_kernel(pupil_ref, same_ref, cross_ref, pair_ref):
    bands, _, rows = same_ref.shape[1:4]
    low_half = low_lanes(rows)

    @pl.loop(0, bands)
    def _(band):
        for group in range(pupil_ref.shape[2] // LANES):
            for part in range(2):
                chosen = pupil_ref[part, pl.ds(band * 2 * rows, 2 * rows), pl.ds(group * LANES, LANES)]
                pair_ref[group, part] = move_lanes(chosen, lane_order())
            for half in range(2):
                chosen = pl.ds(half, rows, stride=2)
                real = pair_ref[group, 0, chosen]
                imag = pair_ref[group, 1, chosen]
                left, right = pack_pair(real, real, low_half)
                same_ref[half, band, 2 * group] = left
                same_ref[half, band, 2 * group + 1] = right
                left, right = pack_pair(-imag, imag, low_half)
                cross_ref[half, band, 2 * group] = left
                cross_ref[half, band, 2 * group + 1] = right


def select_kernel(place_ref, starts_ref, *refs):
    near, outs, rows_ref = refs[:4], refs[4:12], refs[12]
    blocks = near[0].shape[2]
    for source in range(4):
        first = CORES * lax.rem(place_ref[NEAR] + 4 - source, 4)
        for part in range(near[0].shape[0]):
            rows_ref[pl.ds(first, CORES), pl.ds(part * blocks, blocks)] = near[source][part]
    span = outs[0].shape[1]
    for peer in range(len(outs)):
        for row in range(rows_ref.shape[0]):
            outs[peer][row] = rows_ref[row, pl.ds(starts_ref[peer, row], span)]


def table_dot(left, right):
    return jnp.dot(left, right, preferred_element_type=jnp.float32)


def rows_of(place_ref, source, side, row):
    even = place_ref[CORE] == side
    band = CORES * lax.rem(place_ref[HEIGHT] + HEIGHTS - source, HEIGHTS) + lax.rem(row, CORES)
    step = lax.rem(row // CORES + DEPTHS - place_ref[DEPTH], DEPTHS)
    return (
        jnp.where(even, (DEPTHS - source) % DEPTHS, step),
        jnp.where(even, 0, 1),
        jnp.where(even, row, band),
    )


def block_lanes(rows):
    return lax.broadcasted_iota(jnp.int32, (rows, LANES), 1) % (LANES // 2) < LANES // 4


def columns_in(place_ref, source, windows, same_ref, cross_ref, spread_ref, packed_ref, stacked_ref):
    bands, blocks, rows = windows[0].shape[:3]
    taken = bands * rows
    even_lanes = block_lanes(rows)
    for side in range(CORES):
        for row in range(bands):
            _, half, band = rows_of(place_ref, source, side, row)
            place = pl.ds(side * taken + row * rows, rows)
            for pair in range(blocks // 2):
                waves = []
                for block in (2 * pair, 2 * pair + 1):
                    window = windows[side][row, block].astype(jnp.float32)
                    wave = same_ref[half, band, block] * window
                    wave += cross_ref[half, band, block] * swap_halves(window)
                    waves.append(wave)
                lanes = pl.ds(pair * LANES, LANES)
                even = jnp.where(even_lanes, waves[0], pltpu.roll(waves[1], LANES // 4, 1))
                odd = jnp.where(even_lanes, pltpu.roll(waves[0], LANES - LANES // 4, 1), waves[1])
                packed_ref[0, place, lanes] = even.astype(jnp.bfloat16)
                packed_ref[1, place, lanes] = odd.astype(jnp.bfloat16)

    for parity in range(2):
        for part in range(2):
            lanes = pl.ds(part * taken, taken)
            product = table_dot(packed_ref[parity], spread_ref[0, :, lanes])
            product += table_dot(packed_ref[parity], spread_ref[1, :, lanes])
            product = product.astype(jnp.bfloat16)
            for side in range(CORES):
                for row in range(bands):
                    step, half, band = rows_of(place_ref, source, side, row)
                    place = pl.ds(pl.multiple_of(part * taken + band * rows, rows), rows)
                    start = side * taken + row * rows
                    stacked_ref[step, parity, half, place] = product[start:start + rows]


def columns_out(place_ref, source, outs, same_ref, cross_ref, gather_ref, spectral_ref, packed_ref):
    bands, blocks, rows = outs[0].shape[:3]
    taken = bands * rows
    even_lanes = block_lanes(rows)
    for side in range(CORES):
        for row in range(bands):
            step, half, band = rows_of(place_ref, source, side, row)
            place = pl.ds(pl.multiple_of(half * taken + band * rows, rows), rows)
            start = side * taken + row * rows
            for parity in range(2):
                packed_ref[parity, start:start + rows] = spectral_ref[step, parity, place]
    for tile in range(2):
        lanes = pl.ds(tile * TILE, TILE)
        products = []
        for parity in range(2):
            product = table_dot(packed_ref[parity], gather_ref[0, :, lanes])
            products.append(product + table_dot(packed_ref[parity], gather_ref[1, :, lanes]))
        for side in range(CORES):
            for row in range(bands):
                _, half, band = rows_of(place_ref, source, side, row)
                start = side * taken + row * rows
                for inner in range(TILE // LANES):
                    pair = tile * (TILE // LANES) + inner
                    even, odd = (
                        product[start:start + rows, inner * LANES:(inner + 1) * LANES]
                        for product in products
                    )
                    left = jnp.where(even_lanes, even, pltpu.roll(odd, LANES // 4, 1))
                    right = jnp.where(even_lanes, pltpu.roll(even, LANES - LANES // 4, 1), odd)
                    for block, spectral in ((2 * pair, left), (2 * pair + 1, right)):
                        update = same_ref[half, band, block] * spectral
                        update += cross_ref[half, band, block] * swap_halves(spectral)
                        outs[side][row, block] = update.astype(jnp.bfloat16)


def first_kernel(place_ref, *refs):
    count = len(EARLY)
    windows, (same_ref, cross_ref, spread_ref) = refs[:2 * count], refs[2 * count:2 * count + 3]
    stacked_ref, packed_ref = refs[2 * count + 3:]
    for index, source in enumerate(EARLY):
        columns_in(
            place_ref, source, windows[2 * index:2 * index + 2], same_ref, cross_ref, spread_ref,
            packed_ref, stacked_ref,
        )


def last_kernel(place_ref, spectral_ref, same_ref, cross_ref, gather_ref, *refs):
    outs, packed_ref = refs[:-1], refs[-1]
    for index, source in enumerate(EARLY):
        columns_out(
            place_ref, source, outs[2 * index:2 * index + 2], same_ref, cross_ref, gather_ref,
            spectral_ref, packed_ref,
        )


def led_kernel(
    place_ref, leds_ref, early_ref, window0_ref, window1_ref, window2_ref, window3_ref, measured_ref,
    same_ref, cross_ref, rows_ref, spread_ref, gather_ref, down_ref, across_ref,
    update0_ref, update1_ref, update2_ref, update3_ref, spectral_ref, stacked_ref, packed_ref,
):
    steps = stacked_ref.shape[0]
    half_size = stacked_ref.shape[4]
    stacked_ref[...] = early_ref[...]
    windows = (window0_ref, window1_ref), (window2_ref, window3_ref)
    for source, pair in zip(LATE, windows):
        columns_in(place_ref, source, pair, same_ref, cross_ref, spread_ref, packed_ref, stacked_ref)

    turn_re = jnp.concatenate([down_ref[0]] * (half_size // LANES), axis=1)
    turn_im = jnp.concatenate([down_ref[1]] * (half_size // LANES), axis=1)
    down, across = (turn_re, turn_im), (across_ref[0, 0:1], across_ref[1, 0:1])

    def turned(pair, by):
        return pair[0] * by[0] - pair[1] * by[1], pair[0] * by[1] + pair[1] * by[0]

    def plus(left, right):
        return left[0] + right[0], left[1] + right[1]

    def minus(left, right):
        return left[0] - right[0], left[1] - right[1]

    @pl.loop(0, steps)
    def _(step):
        led = leds_ref[step]

        def row_transform(half, parity):
            moved = table_dot(rows_ref[0], stacked_ref[step, parity, half])
            moved += table_dot(rows_ref[1], stacked_ref[step, parity, half])
            return moved[:half_size], moved[half_size:]

        def residual(field, row, lane):
            measured = measured_ref[led, pl.ds(row, half_size), pl.ds(lane, half_size)]
            real, imag = field
            factor = 1.0 - measured * lax.rsqrt(real * real + imag * imag + floor_sq)
            return real * factor, -imag * factor

        tops, lows = [], []
        for parity in range(2):
            first = row_transform(0, parity)
            second = turned(row_transform(1, parity), down)
            tops.append(plus(first, second))
            lows.append(minus(first, second))
        parts = []
        for row, (first, second) in ((0, tops), (half_size, lows)):
            second = turned(second, across)
            left = residual(plus(first, second), row, 0)
            right = residual(minus(first, second), row, half_size)
            parts.append((plus(left, right), turned(minus(left, right), across)))
        for parity in range(2):
            top, low = parts[0][parity], parts[1][parity]
            for half, value in enumerate((plus(top, low), turned(minus(top, low), down))):
                for part in range(2):
                    stacked_ref[step, parity, half, pl.ds(part * half_size, half_size)] = value[
                        part
                    ].astype(jnp.bfloat16)
        for parity in range(2):
            for half in range(2):
                moved = row_transform(half, parity)
                for part in range(2):
                    spectral_ref[
                        step, parity, pl.ds(half * half_size, half_size), pl.ds(part * half_size, half_size)
                    ] = moved[part].astype(jnp.bfloat16)

    updates = (update0_ref, update1_ref), (update2_ref, update3_ref)
    for source, pair in zip(LATE, updates):
        columns_out(place_ref, source, pair, same_ref, cross_ref, gather_ref, spectral_ref, packed_ref)


def collect_kernel(place_ref, starts_ref, *refs):
    updates, outs, total_ref = refs[:8], refs[8:12], refs[12]
    span = updates[0].shape[1]
    for peer in range(4):
        first = CORES * lax.rem(place_ref[NEAR] + peer, 4)
        for side in range(CORES):
            total_ref[...] = jnp.zeros_like(total_ref)
            for source in range(8):
                place = pl.ds(starts_ref[source, first + side], span)
                total_ref[place] = total_ref[place] + updates[source][first + side].astype(jnp.float32)
            outs[peer][side] = total_ref[...].astype(outs[peer].dtype)


def columns_kernel(place_ref, *refs):
    parts, outs = refs[:4], refs[4:]
    blocks = outs[0].shape[1]
    for peer in range(len(outs)):
        place = pl.ds(lax.rem(place_ref[COLUMN] + peer, len(outs)) * blocks, blocks)
        for side in range(CORES):
            total = parts[0][side, place].astype(jnp.float32)
            for part in parts[1:]:
                total = total + part[side, place].astype(jnp.float32)
            outs[peer][side] = total.astype(outs[peer].dtype)


def halves_kernel(place_ref, part0_ref, part1_ref, part2_ref, part3_ref, keep_ref, send_ref):
    core = place_ref[CORE]
    for out_ref, side in ((keep_ref, core), (send_ref, 1 - core)):
        total = part0_ref[side].astype(jnp.float32)
        for part_ref in (part1_ref, part2_ref, part3_ref):
            total = total + part_ref[side].astype(jnp.float32)
        out_ref[...] = total


def final_kernel(place_ref, own_ref, other_ref, spectrum_ref, out_ref, pair_ref):
    rows, width = spectrum_ref.shape[1:]
    low_half = low_lanes(rows // 2)
    first_core = place_ref[CORE] == 0
    back = lane_order(back=True)
    for group in range(width // LANES):
        for half in range(2):
            sums = []
            for block in (2 * group, 2 * group + 1):
                pair = (own_ref[block], other_ref[block])
                sums.append(jnp.where(first_core, pair[half], pair[1 - half]))
            real, imag = pack_pair(sums[0], sums[1], low_half)
            chosen = pl.ds(half, rows // 2, stride=2)
            pair_ref[group, 0, chosen] = -step_size * real
            pair_ref[group, 1, chosen] = step_size * imag
        lanes = pl.ds(group * LANES, LANES)
        for part in range(2):
            step = move_lanes(pair_ref[group, part], back)
            out_ref[part, :, lanes] = spectrum_ref[part, :, lanes] + step


def call(kernel, outs, inputs, mib, name, scalars=0, scratch=(), flops=0):
    size = sum(math.prod(out.shape) * out.dtype.itemsize for out in outs)
    size += sum(math.prod(array.shape) * array.dtype.itemsize for array in inputs)
    return pl.pallas_call(
        kernel,
        out_shape=tuple(outs),
        in_specs=[SMEM] * scalars + [VMEM] * (len(inputs) - scalars),
        out_specs=(VMEM,) * len(outs),
        scratch_shapes=list(scratch),
        compiler_params=params(mib),
        cost_estimate=pl.CostEstimate(flops=flops, bytes_accessed=size, transcendentals=0),
        name=name,
    )(*inputs)


TILES = DEPTHS * HEIGHTS * CORES


def tile_of(depth, height, core):
    return (depth % DEPTHS * HEIGHTS + height % HEIGHTS) * CORES + core


def tile_moves(even_move, odd_move):
    pairs = []
    for tile in range(TILES):
        depth, height, core = tile // (HEIGHTS * CORES), tile // CORES % HEIGHTS, tile % CORES
        pairs.append((tile, tile_of(*(odd_move if core else even_move)(depth, height))))
    return pairs


def far_moves(steps, side):
    return tile_moves(
        lambda depth, height: (depth + steps, height, side),
        lambda depth, height: (depth, height + steps, 1 - side),
    )


def near_moves(steps):
    return tile_moves(
        lambda depth, height: (depth, height + steps, 0),
        lambda depth, height: (depth + steps, height, 1),
    )


def reverse(moves):
    return [(target, source) for source, target in moves]


def send(array, moves, axis="tile"):
    return lax.ppermute(array, axis, moves)


def on_device(spectrum, pupil_field, amplitude, offsets):
    columns = lax.axis_size("col")
    tile, column = lax.axis_index("tile"), lax.axis_index("col")
    depth, height, core = tile // (HEIGHTS * CORES), tile // CORES % HEIGHTS, tile % CORES
    block_rows, own_width = spectrum.shape[1:]
    size = pupil_field.shape[1]
    span = size // block_rows
    own_blocks = own_width // block_rows
    band_blocks = own_blocks * columns
    rows = block_rows // 2
    bf16, f32 = jnp.bfloat16, jnp.float32
    shaped = lambda *shape, dtype=bf16: jax.ShapeDtypeStruct(shape, dtype)
    near = jnp.where(core == 0, height, depth)
    place = jnp.stack([depth, height, core, column, near]).astype(jnp.int32)
    swap = [(t, t ^ 1) for t in range(TILES)]

    wanted = jnp.arange(DEPTHS, dtype=jnp.int32) * span
    mine = offsets[None, :, 0] == wanted[:, None]
    slots = jnp.arange(offsets.shape[0], dtype=jnp.int32)[None]
    leds = jnp.roll(jnp.sum(jnp.where(mine, slots, 0), axis=1), -depth).astype(jnp.int32)
    firsts = jnp.sum(jnp.where(mine, offsets[None, :, 1], 0), axis=1).astype(jnp.int32)
    chip = jnp.stack([firsts, send(firsts, swap)])
    chips = jnp.stack([chip] + [send(chip, reverse(far_moves(steps, 0))) for steps in range(1, 4)])
    by_row = jnp.repeat(chips, CORES, axis=2)
    same_band = jnp.broadcast_to(lax.dynamic_slice_in_dim(chips, depth, 1, 2), by_row.shape)
    starts = jnp.where(core == 0, same_band, by_row).reshape(8, span).astype(jnp.int32)

    pairs = lambda width: [pltpu.VMEM((width // LANES, 2, block_rows, LANES), f32)]
    part_shape = (own_blocks, rows, LANES)
    tables = [jnp.asarray(table) for table in dft_tables(size, block_rows)]
    keep, give = call(
        prep_kernel,
        [shaped(*part_shape)] * 2,
        [place, spectrum],
        4,
        "prep",
        scalars=1,
        scratch=pairs(own_width),
    )
    joined, = call(
        join_kernel, [shaped(CORES, *part_shape)], [place, keep, send(give, swap)], 2, "join", scalars=1
    )
    band = lax.all_gather(joined, "col", axis=0)
    near_parts = [band] + [send(band, near_moves(steps)) for steps in range(1, 4)]
    windows = call(
        select_kernel,
        [shaped(span, span, rows, LANES)] * 8,
        [place, starts] + near_parts,
        6,
        "select",
        scalars=2,
        scratch=[pltpu.VMEM((span, band_blocks, rows, LANES), bf16)],
    )
    far = [far_moves(steps, side) for steps in range(4) for side in range(CORES)]
    early = [2 * source + side for source in EARLY for side in range(CORES)]
    late = [2 * source + side for source in LATE for side in range(CORES)]
    incoming = [send(windows[peer], far[peer]) if peer else windows[0] for peer in early]
    late_windows = [send(windows[peer], far[peer]) for peer in late]

    pupil_shape = shaped(2, span, span, rows, LANES, dtype=f32)
    same, cross = call(pupil_kernel, [pupil_shape] * 2, [pupil_field], 4, "pupil", scratch=pairs(size))
    stacked_shape = (DEPTHS, 2, 2, size, size // 2)
    packed_scratch = pltpu.VMEM((2, size, size), bf16)
    window_shape = shaped(span, span, rows, LANES)
    rows_table, spread, gather, down, across = tables
    stacked, = call(
        first_kernel,
        [shaped(*stacked_shape)],
        [place, *incoming, same, cross, spread],
        12,
        "first",
        scalars=1,
        scratch=[packed_scratch],
        flops=48 * size**3,
    )
    *late_updates, spectral = call(
        led_kernel,
        [window_shape] * len(late) + [shaped(DEPTHS, 2, size, size)],
        [place, leds, stacked, *late_windows]
        + [amplitude, same, cross, rows_table, spread, gather, down, across],
        16,
        "leds",
        scalars=2,
        scratch=[pltpu.VMEM(stacked_shape, bf16), packed_scratch],
        flops=128 * size**3,
    )
    rest = call(
        last_kernel,
        [window_shape] * len(early),
        [place, spectral, same, cross, gather],
        12,
        "last",
        scalars=1,
        scratch=[packed_scratch],
        flops=48 * size**3,
    )
    late_returned = [send(update, reverse(far[peer])) for update, peer in zip(late_updates, late)]
    rest, late_returned[0] = lax.optimization_barrier((list(rest), late_returned[0]))
    returned = [None] * 8
    for peer, update in zip(late + early, late_returned + rest):
        returned[peer] = update if peer in late or not peer else send(update, reverse(far[peer]))

    sum_shape = (CORES, band_blocks, rows, LANES)
    sums = call(
        collect_kernel,
        [shaped(*sum_shape, dtype=f32)] + [shaped(*sum_shape)] * 3,
        [place, starts] + returned,
        4,
        "collect",
        scalars=2,
        scratch=[pltpu.VMEM(sum_shape[1:], f32)],
    )
    near_sums = [sums[0]] + [send(sums[steps], near_moves(steps)) for steps in range(1, 4)]
    cut = call(
        columns_kernel,
        [shaped(CORES, *part_shape, dtype=f32)] + [shaped(CORES, *part_shape)] * (columns - 1),
        [place] + near_sums,
        4,
        "columns",
        scalars=1,
    )
    along = lambda steps: [(c, (c + steps) % columns) for c in range(columns)]
    parts = [cut[0]] + [send(cut[steps], along(steps), "col") for steps in range(1, columns)]
    keep, give = call(
        halves_kernel, [shaped(*part_shape, dtype=f32)] * 2, [place] + parts, 2, "halves", scalars=1
    )
    return call(
        final_kernel,
        [shaped(*spectrum.shape, dtype=f32)],
        [place, keep, send(give, swap), spectrum],
        4,
        "final",
        scalars=1,
        scratch=pairs(own_width),
    )[0]


def solution(mesh):
    in_specs = (
        P(None, "tile", "col"),
        P(),
        P(("tile", "col"), None, None),
        P(("tile", "col"), None),
    )
    return jax.shard_map(
        on_device, mesh=mesh, in_specs=in_specs, out_specs=P(None, "tile", "col"), check_vma=False
    )
```

```python
import math

import jax
import jax.numpy as jnp
import numpy as np
from jax import lax
from jax.experimental import pallas as pl
from jax.experimental.pallas import tpu as pltpu
from jax.sharding import PartitionSpec as P

floor_sq = 0.25
step_size = 0.5
LANES = 128
DEPTHS, HEIGHTS, CORES = 4, 4, 2
TILE = 256
EARLY, LATE = (2, 0), (1, 3)
DEPTH, HEIGHT, CORE, COLUMN, NEAR = range(5)
VMEM = pl.BlockSpec(memory_space=pltpu.VMEM)
SMEM = pl.BlockSpec(memory_space=pltpu.SMEM)


def params(mib, **more):
    return pltpu.CompilerParams(vmem_limit_bytes=mib * 2**20, **more)


def split_table(table):
    high = table.astype(jnp.bfloat16)
    low = (table - high.astype(np.float64)).astype(jnp.bfloat16)
    return np.stack([high, low])


def dft_tables(length, block):
    half = length // 2
    counter = np.arange(half)
    angles = (counter[:, None] * counter[None, :] % half) * (2.0 * math.pi / half)
    cosine = np.cos(angles) / math.sqrt(length)
    sine = np.sin(angles) / math.sqrt(length)
    rows = np.block([[cosine, -sine], [sine, cosine]])
    right = np.block([[cosine, sine], [-sine, cosine]])
    pairs = length // (2 * block)
    lanes = np.arange(length).reshape(2, pairs, block).transpose(1, 0, 2).reshape(-1)
    turn = np.arange(half) * (2.0 * math.pi / length)
    turn = np.stack([np.cos(turn), np.sin(turn)])
    down = np.broadcast_to(turn[:, :, None], (2, half, LANES)).astype(np.float32)
    across = np.broadcast_to(turn[:, None, :], (2, 8, half)).astype(np.float32)
    tables = split_table(rows), split_table(right[lanes]), split_table(right[:, lanes])
    return *tables, down, across


def swap_halves(packed):
    return pltpu.roll(packed, LANES // 2, axis=packed.ndim - 1)


def pack_pair(first, second, low_half):
    left = jnp.where(low_half, first, swap_halves(second))
    right = jnp.where(low_half, swap_halves(first), second)
    return left, right


def lane_order(back=False):
    row = lax.broadcasted_iota(jnp.int32, (LANES, LANES), 0)
    column = lax.broadcasted_iota(jnp.int32, (LANES, LANES), 1)
    plain, moved = (column, row) if back else (row, column)
    block = LANES // 2
    inner = moved % block
    source = moved - inner + 2 * (inner % (block // 2)) + inner // (block // 2)
    return jnp.where(plain == source, 1.0, 0.0).astype(jnp.bfloat16)


def move_lanes(values, order):
    total = None
    for _ in range(3):
        part = values.astype(jnp.bfloat16)
        values = values - part.astype(jnp.float32)
        moved = jnp.dot(part, order, preferred_element_type=jnp.float32)
        total = moved if total is None else total + moved
    return total


def low_lanes(rows):
    return lax.broadcasted_iota(jnp.int32, (rows, LANES), 1) < LANES // 2


def prep_kernel(place_ref, spectrum_ref, keep_ref, send_ref, pair_ref):
    rows, width = spectrum_ref.shape[1:]
    low_half = low_lanes(rows // 2)
    first_core = place_ref[CORE] == 0
    order = lane_order()
    for group in range(width // LANES):
        for part in range(2):
            rounded = spectrum_ref[part, :, pl.ds(group * LANES, LANES)].astype(jnp.bfloat16)
            pair_ref[group, part] = jnp.dot(rounded, order, preferred_element_type=jnp.float32)
        halves = []
        for half in range(2):
            chosen = pl.ds(half, rows // 2, stride=2)
            halves.append(pack_pair(pair_ref[group, 0, chosen], pair_ref[group, 1, chosen], low_half))
        for side in range(2):
            even, odd = halves[0][side], halves[1][side]
            block = 2 * group + side
            keep_ref[block] = jnp.where(first_core, even, odd).astype(jnp.bfloat16)
            send_ref[block] = jnp.where(first_core, odd, even).astype(jnp.bfloat16)


def join_kernel(place_ref, own_ref, other_ref, out_ref):
    core = place_ref[CORE]
    out_ref[core] = own_ref[...]
    out_ref[1 - core] = other_ref[...]


def pupil_kernel(pupil_ref, same_ref, cross_ref, pair_ref):
    bands, _, rows = same_ref.shape[1:4]
    low_half = low_lanes(rows)
    order = lane_order()
    for group in range(pupil_ref.shape[2] // LANES):
        for part in range(2):
            chosen = pupil_ref[part, :, pl.ds(group * LANES, LANES)]
            pair_ref[group, part] = move_lanes(chosen, order)
        for half in range(2):
            for band in range(bands):
                chosen = pl.ds(band * 2 * rows + half, rows, stride=2)
                real, imag = pair_ref[group, 0, chosen], pair_ref[group, 1, chosen]
                left, right = pack_pair(real, real, low_half)
                same_ref[half, band, 2 * group] = left
                same_ref[half, band, 2 * group + 1] = right
                left, right = pack_pair(-imag, imag, low_half)
                cross_ref[half, band, 2 * group] = left
                cross_ref[half, band, 2 * group + 1] = right


def select_kernel(place_ref, starts_ref, *refs):
    near, outs, rows_ref = refs[:4], refs[4:12], refs[12]
    blocks = near[0].shape[2]
    for source in range(4):
        first = CORES * lax.rem(place_ref[NEAR] + 4 - source, 4)
        for part in range(near[0].shape[0]):
            rows_ref[pl.ds(first, CORES), pl.ds(part * blocks, blocks)] = near[source][part]
    span = outs[0].shape[1]
    for peer in range(len(outs)):
        for row in range(rows_ref.shape[0]):
            outs[peer][row] = rows_ref[row, pl.ds(starts_ref[peer, row], span)]


def table_dot(left, right):
    return jnp.dot(left, right, preferred_element_type=jnp.float32)


def rows_of(place_ref, source, side, row):
    even = place_ref[CORE] == side
    band = CORES * lax.rem(place_ref[HEIGHT] + HEIGHTS - source, HEIGHTS) + lax.rem(row, CORES)
    step = lax.rem(row // CORES + DEPTHS - place_ref[DEPTH], DEPTHS)
    return (
        jnp.where(even, (DEPTHS - source) % DEPTHS, step),
        jnp.where(even, 0, 1),
        jnp.where(even, row, band),
    )


def block_lanes(rows):
    return lax.broadcasted_iota(jnp.int32, (rows, LANES), 1) % (LANES // 2) < LANES // 4


def columns_in(place_ref, source, windows, same_ref, cross_ref, spread_ref, packed_ref, stacked_ref):
    bands, blocks, rows = windows[0].shape[:3]
    taken = bands * rows
    even_lanes = block_lanes(rows)
    for side in range(CORES):
        for row in range(bands):
            _, half, band = rows_of(place_ref, source, side, row)
            place = pl.ds(side * taken + row * rows, rows)
            for pair in range(blocks // 2):
                waves = []
                for block in (2 * pair, 2 * pair + 1):
                    window = windows[side][row, block]
                    wave = same_ref[half, band, block] * window.astype(jnp.float32)
                    wave += cross_ref[half, band, block] * swap_halves(window).astype(jnp.float32)
                    waves.append(wave.astype(jnp.bfloat16))
                lanes = pl.ds(pair * LANES, LANES)
                even = jnp.where(even_lanes, waves[0], pltpu.roll(waves[1], LANES // 4, 1))
                odd = jnp.where(even_lanes, pltpu.roll(waves[0], LANES - LANES // 4, 1), waves[1])
                packed_ref[0, place, lanes] = even
                packed_ref[1, place, lanes] = odd

    for parity in range(2):
        for part in range(2):
            lanes = pl.ds(part * taken, taken)
            product = table_dot(packed_ref[parity], spread_ref[0, :, lanes])
            product += table_dot(packed_ref[parity], spread_ref[1, :, lanes])
            product = product.astype(jnp.bfloat16)
            for side in range(CORES):
                for row in range(bands):
                    step, half, band = rows_of(place_ref, source, side, row)
                    place = pl.ds(pl.multiple_of(part * taken + band * rows, rows), rows)
                    start = side * taken + row * rows
                    stacked_ref[step, parity, half, place] = product[start:start + rows]


def columns_out(place_ref, source, outs, same_ref, cross_ref, gather_ref, spectral_ref, packed_ref):
    bands, blocks, rows = outs[0].shape[:3]
    taken = bands * rows
    even_lanes = block_lanes(rows)
    for side in range(CORES):
        for row in range(bands):
            step, half, band = rows_of(place_ref, source, side, row)
            place = pl.ds(pl.multiple_of(half * taken + band * rows, rows), rows)
            start = side * taken + row * rows
            for parity in range(2):
                packed_ref[parity, start:start + rows] = spectral_ref[step, parity, place]
    for tile in range(2):
        lanes = pl.ds(tile * TILE, TILE)
        products = []
        for parity in range(2):
            product = table_dot(packed_ref[parity], gather_ref[0, :, lanes])
            products.append(product + table_dot(packed_ref[parity], gather_ref[1, :, lanes]))
        for side in range(CORES):
            for row in range(bands):
                _, half, band = rows_of(place_ref, source, side, row)
                start = side * taken + row * rows
                for inner in range(TILE // LANES):
                    pair = tile * (TILE // LANES) + inner
                    even, odd = (
                        product[start:start + rows, inner * LANES:(inner + 1) * LANES]
                        for product in products
                    )
                    left = jnp.where(even_lanes, even, pltpu.roll(odd, LANES // 4, 1))
                    right = jnp.where(even_lanes, pltpu.roll(even, LANES - LANES // 4, 1), odd)
                    for block, spectral in ((2 * pair, left), (2 * pair + 1, right)):
                        update = same_ref[half, band, block] * spectral
                        update += cross_ref[half, band, block] * swap_halves(spectral)
                        outs[side][row, block] = update.astype(jnp.bfloat16)


def first_kernel(place_ref, *refs):
    count = len(EARLY)
    windows, (same_ref, cross_ref, spread_ref) = refs[:2 * count], refs[2 * count:2 * count + 3]
    stacked_ref, packed_ref = refs[2 * count + 3:]
    for index, source in enumerate(EARLY):
        columns_in(
            place_ref, source, windows[2 * index:2 * index + 2], same_ref, cross_ref, spread_ref,
            packed_ref, stacked_ref,
        )


def last_kernel(place_ref, spectral_ref, same_ref, cross_ref, gather_ref, *refs):
    outs, packed_ref = refs[:-1], refs[-1]
    for index, source in enumerate(LATE):
        columns_out(
            place_ref, source, outs[2 * index:2 * index + 2], same_ref, cross_ref, gather_ref,
            spectral_ref, packed_ref,
        )


def led_kernel(
    place_ref, leds_ref, early_ref, window0_ref, window1_ref, window2_ref, window3_ref, measured_ref,
    same_ref, cross_ref, rows_ref, spread_ref, gather_ref, down_ref, across_ref,
    update0_ref, update1_ref, update2_ref, update3_ref, spectral_ref, stacked_ref, packed_ref,
):
    steps = stacked_ref.shape[0]
    half_size = stacked_ref.shape[4]
    stacked_ref[...] = early_ref[...]
    windows = (window0_ref, window1_ref), (window2_ref, window3_ref)
    for source, pair in zip(LATE, windows):
        columns_in(place_ref, source, pair, same_ref, cross_ref, spread_ref, packed_ref, stacked_ref)

    turn_re = jnp.concatenate([down_ref[0]] * (half_size // LANES), axis=1)
    turn_im = jnp.concatenate([down_ref[1]] * (half_size // LANES), axis=1)
    down, across = (turn_re, turn_im), (across_ref[0, 0:1], across_ref[1, 0:1])

    def turned(pair, by):
        return pair[0] * by[0] - pair[1] * by[1], pair[0] * by[1] + pair[1] * by[0]

    def plus(left, right):
        return left[0] + right[0], left[1] + right[1]

    def minus(left, right):
        return left[0] - right[0], left[1] - right[1]

    @pl.loop(0, steps)
    def _(step):
        led = leds_ref[step]

        def row_transform(half, parity):
            moved = table_dot(rows_ref[0], stacked_ref[step, parity, half])
            moved += table_dot(rows_ref[1], stacked_ref[step, parity, half])
            return moved[:half_size], moved[half_size:]

        def residual(field, row, lane):
            measured = measured_ref[led, pl.ds(row, half_size), pl.ds(lane, half_size)]
            real, imag = field
            factor = 1.0 - measured * lax.rsqrt(real * real + imag * imag + floor_sq)
            return real * factor, -imag * factor

        tops, lows = [], []
        for parity in range(2):
            first = row_transform(0, parity)
            second = turned(row_transform(1, parity), down)
            tops.append(plus(first, second))
            lows.append(minus(first, second))
        parts = []
        for row, (first, second) in ((0, tops), (half_size, lows)):
            second = turned(second, across)
            left = residual(plus(first, second), row, 0)
            right = residual(minus(first, second), row, half_size)
            parts.append((plus(left, right), turned(minus(left, right), across)))
        for parity in range(2):
            top, low = parts[0][parity], parts[1][parity]
            for half, value in enumerate((plus(top, low), turned(minus(top, low), down))):
                for part in range(2):
                    stacked_ref[step, parity, half, pl.ds(part * half_size, half_size)] = value[
                        part
                    ].astype(jnp.bfloat16)
        for parity in range(2):
            for half in range(2):
                moved = row_transform(half, parity)
                for part in range(2):
                    spectral_ref[
                        step, parity, pl.ds(half * half_size, half_size), pl.ds(part * half_size, half_size)
                    ] = moved[part].astype(jnp.bfloat16)

    updates = (update0_ref, update1_ref), (update2_ref, update3_ref)
    for source, pair in zip(EARLY, updates):
        columns_out(place_ref, source, pair, same_ref, cross_ref, gather_ref, spectral_ref, packed_ref)


def collect_kernel(place_ref, starts_ref, *refs):
    updates, outs, total_ref = refs[:8], refs[8:12], refs[12]
    span = updates[0].shape[1]
    for peer in range(4):
        first = CORES * lax.rem(place_ref[NEAR] + peer, 4)
        for side in range(CORES):
            total_ref[...] = jnp.zeros_like(total_ref)
            for source in range(8):
                place = pl.ds(starts_ref[source, first + side], span)
                total_ref[place] = total_ref[place] + updates[source][first + side].astype(jnp.float32)
            outs[peer][side] = total_ref[...].astype(outs[peer].dtype)


def columns_kernel(place_ref, *refs):
    parts, outs = refs[:4], refs[4:]
    blocks = outs[0].shape[1]
    for peer in range(len(outs)):
        place = pl.ds(lax.rem(place_ref[COLUMN] + peer, len(outs)) * blocks, blocks)
        for side in range(CORES):
            total = parts[0][side, place].astype(jnp.float32)
            for part in parts[1:]:
                total = total + part[side, place].astype(jnp.float32)
            outs[peer][side] = total.astype(outs[peer].dtype)


def halves_kernel(place_ref, part0_ref, part1_ref, part2_ref, part3_ref, keep_ref, send_ref):
    core = place_ref[CORE]
    for out_ref, side in ((keep_ref, core), (send_ref, 1 - core)):
        total = part0_ref[side].astype(jnp.float32)
        for part_ref in (part1_ref, part2_ref, part3_ref):
            total = total + part_ref[side].astype(jnp.float32)
        out_ref[...] = total


def final_kernel(place_ref, own_ref, other_ref, spectrum_ref, out_ref, pair_ref):
    rows, width = spectrum_ref.shape[1:]
    low_half = low_lanes(rows // 2)
    first_core = place_ref[CORE] == 0
    back = lane_order(back=True)
    for group in range(width // LANES):
        for half in range(2):
            sums = []
            for block in (2 * group, 2 * group + 1):
                pair = (own_ref[block], other_ref[block])
                sums.append(jnp.where(first_core, pair[half], pair[1 - half]))
            real, imag = pack_pair(sums[0], sums[1], low_half)
            chosen = pl.ds(half, rows // 2, stride=2)
            pair_ref[group, 0, chosen] = -step_size * real
            pair_ref[group, 1, chosen] = step_size * imag
        lanes = pl.ds(group * LANES, LANES)
        for part in range(2):
            step = move_lanes(pair_ref[group, part], back)
            out_ref[part, :, lanes] = spectrum_ref[part, :, lanes] + step


def call(kernel, outs, inputs, mib, name, scalars=0, scratch=(), flops=0):
    size = sum(math.prod(out.shape) * out.dtype.itemsize for out in outs)
    size += sum(math.prod(array.shape) * array.dtype.itemsize for array in inputs)
    return pl.pallas_call(
        kernel,
        out_shape=tuple(outs),
        in_specs=[SMEM] * scalars + [VMEM] * (len(inputs) - scalars),
        out_specs=(VMEM,) * len(outs),
        scratch_shapes=list(scratch),
        compiler_params=params(mib),
        cost_estimate=pl.CostEstimate(flops=flops, bytes_accessed=size, transcendentals=0),
        name=name,
    )(*inputs)


TILES = DEPTHS * HEIGHTS * CORES


def tile_of(depth, height, core):
    return (depth % DEPTHS * HEIGHTS + height % HEIGHTS) * CORES + core


def tile_moves(even_move, odd_move):
    pairs = []
    for tile in range(TILES):
        depth, height, core = tile // (HEIGHTS * CORES), tile // CORES % HEIGHTS, tile % CORES
        pairs.append((tile, tile_of(*(odd_move if core else even_move)(depth, height))))
    return pairs


def far_moves(steps, side):
    return tile_moves(
        lambda depth, height: (depth + steps, height, side),
        lambda depth, height: (depth, height + steps, 1 - side),
    )


def near_moves(steps):
    return tile_moves(
        lambda depth, height: (depth, height + steps, 0),
        lambda depth, height: (depth + steps, height, 1),
    )


def reverse(moves):
    return [(target, source) for source, target in moves]


def send(array, moves, axis="tile"):
    return lax.ppermute(array, axis, moves)


def on_device(spectrum, pupil_field, amplitude, offsets):
    columns = lax.axis_size("col")
    tile, column = lax.axis_index("tile"), lax.axis_index("col")
    depth, height, core = tile // (HEIGHTS * CORES), tile // CORES % HEIGHTS, tile % CORES
    block_rows, own_width = spectrum.shape[1:]
    size = pupil_field.shape[1]
    span = size // block_rows
    own_blocks = own_width // block_rows
    band_blocks = own_blocks * columns
    rows = block_rows // 2
    bf16, f32 = jnp.bfloat16, jnp.float32
    shaped = lambda *shape, dtype=bf16: jax.ShapeDtypeStruct(shape, dtype)
    near = jnp.where(core == 0, height, depth)
    place = jnp.stack([depth, height, core, column, near]).astype(jnp.int32)
    swap = [(t, t ^ 1) for t in range(TILES)]

    wanted = jnp.arange(DEPTHS, dtype=jnp.int32) * span
    mine = offsets[None, :, 0] == wanted[:, None]
    slots = jnp.arange(offsets.shape[0], dtype=jnp.int32)[None]
    leds = jnp.roll(jnp.sum(jnp.where(mine, slots, 0), axis=1), -depth).astype(jnp.int32)
    firsts = jnp.sum(jnp.where(mine, offsets[None, :, 1], 0), axis=1).astype(jnp.int32)
    chip = jnp.stack([firsts, send(firsts, swap)])
    chips = jnp.stack([chip] + [send(chip, reverse(far_moves(steps, 0))) for steps in range(1, 4)])
    by_row = jnp.repeat(chips, CORES, axis=2)
    same_band = jnp.broadcast_to(lax.dynamic_slice_in_dim(chips, depth, 1, 2), by_row.shape)
    starts = jnp.where(core == 0, same_band, by_row).reshape(8, span).astype(jnp.int32)

    pairs = lambda width: [pltpu.VMEM((width // LANES, 2, block_rows, LANES), f32)]
    part_shape = (own_blocks, rows, LANES)
    tables = [jnp.asarray(table) for table in dft_tables(size, block_rows)]
    keep, give = call(
        prep_kernel,
        [shaped(*part_shape)] * 2,
        [place, spectrum],
        4,
        "prep",
        scalars=1,
        scratch=pairs(own_width),
    )
    joined, = call(
        join_kernel, [shaped(CORES, *part_shape)], [place, keep, send(give, swap)], 2, "join", scalars=1
    )
    band = lax.all_gather(joined, "col", axis=0)
    near_parts = [band] + [send(band, near_moves(steps)) for steps in range(1, 4)]
    windows = call(
        select_kernel,
        [shaped(span, span, rows, LANES)] * 8,
        [place, starts] + near_parts,
        56,
        "select",
        scalars=2,
        scratch=[pltpu.VMEM((span, band_blocks, rows, LANES), bf16)],
    )
    far = [far_moves(steps, side) for steps in range(4) for side in range(CORES)]
    early = [2 * source + side for source in EARLY for side in range(CORES)]
    late = [2 * source + side for source in LATE for side in range(CORES)]
    incoming = [send(windows[peer], far[peer]) if peer else windows[0] for peer in early]
    late_windows = [send(windows[peer], far[peer]) for peer in late]

    pupil_shape = shaped(2, span, span, rows, LANES, dtype=f32)
    same, cross = call(pupil_kernel, [pupil_shape] * 2, [pupil_field], 8, "pupil", scratch=[
        pltpu.VMEM((size // LANES, 2, size, LANES), f32)
    ])
    stacked_shape = (DEPTHS, 2, 2, size, size // 2)
    packed_scratch = pltpu.VMEM((2, size, size), bf16)
    window_shape = shaped(span, span, rows, LANES)
    rows_table, spread, gather, down, across = tables
    stacked, = call(
        first_kernel,
        [shaped(*stacked_shape)],
        [place, *incoming, same, cross, spread],
        12,
        "first",
        scalars=1,
        scratch=[packed_scratch],
        flops=48 * size**3,
    )
    *first_updates, spectral = call(
        led_kernel,
        [window_shape] * len(early) + [shaped(DEPTHS, 2, size, size)],
        [place, leds, stacked, *late_windows]
        + [amplitude, same, cross, rows_table, spread, gather, down, across],
        16,
        "leds",
        scalars=2,
        scratch=[pltpu.VMEM(stacked_shape, bf16), packed_scratch],
        flops=128 * size**3,
    )
    rest = call(
        last_kernel,
        [window_shape] * len(late),
        [place, spectral, same, cross, gather],
        12,
        "last",
        scalars=1,
        scratch=[packed_scratch],
        flops=48 * size**3,
    )
    returned = [None] * 8
    for peer, update in zip(early, first_updates):
        returned[peer] = send(update, reverse(far[peer])) if peer else update
    rest, returned[1] = lax.optimization_barrier((list(rest), returned[1]))
    for peer, update in zip(late, rest):
        returned[peer] = send(update, reverse(far[peer]))

    sum_shape = (CORES, band_blocks, rows, LANES)
    sums = call(
        collect_kernel,
        [shaped(*sum_shape, dtype=f32)] + [shaped(*sum_shape)] * 3,
        [place, starts] + returned,
        4,
        "collect",
        scalars=2,
        scratch=[pltpu.VMEM(sum_shape[1:], f32)],
    )
    near_sums = [sums[0]] + [send(sums[steps], near_moves(steps)) for steps in range(1, 4)]
    cut = call(
        columns_kernel,
        [shaped(CORES, *part_shape, dtype=f32)] + [shaped(CORES, *part_shape)] * (columns - 1),
        [place] + near_sums,
        4,
        "columns",
        scalars=1,
    )
    along = lambda steps: [(c, (c + steps) % columns) for c in range(columns)]
    parts = [cut[0]] + [send(cut[steps], along(steps), "col") for steps in range(1, columns)]
    keep, give = call(
        halves_kernel, [shaped(*part_shape, dtype=f32)] * 2, [place] + parts, 2, "halves", scalars=1
    )
    return call(
        final_kernel,
        [shaped(*spectrum.shape, dtype=f32)],
        [place, keep, send(give, swap), spectrum],
        4,
        "final",
        scalars=1,
        scratch=pairs(own_width),
    )[0]


def solution(mesh):
    in_specs = (
        P(None, "tile", "col"),
        P(),
        P(("tile", "col"), None, None),
        P(("tile", "col"), None),
    )
    return jax.shard_map(
        on_device, mesh=mesh, in_specs=in_specs, out_specs=P(None, "tile", "col"), check_vma=False
    )
```

```python
import math

import jax
import jax.numpy as jnp
import numpy as np
from jax import lax
from jax.experimental import pallas as pl
from jax.experimental.pallas import tpu as pltpu
from jax.sharding import PartitionSpec as P

floor_sq = 0.25
step_size = 0.5
LANES = 128
DEPTHS, HEIGHTS, CORES = 4, 4, 2
TILE = 256
EARLY, LATE = (2, 0), (1, 3)
DEPTH, HEIGHT, CORE, COLUMN, NEAR = range(5)
VMEM = pl.BlockSpec(memory_space=pltpu.VMEM)
SMEM = pl.BlockSpec(memory_space=pltpu.SMEM)


def params(mib, **more):
    return pltpu.CompilerParams(vmem_limit_bytes=mib * 2**20, **more)


def split_table(table):
    high = table.astype(jnp.bfloat16)
    low = (table - high.astype(np.float64)).astype(jnp.bfloat16)
    return np.stack([high, low])


def dft_tables(length, block):
    half = length // 2
    counter = np.arange(half)
    angles = (counter[:, None] * counter[None, :] % half) * (2.0 * math.pi / half)
    cosine = np.cos(angles) / math.sqrt(length)
    sine = np.sin(angles) / math.sqrt(length)
    rows = np.block([[cosine, -sine], [sine, cosine]])
    right = np.block([[cosine, sine], [-sine, cosine]])
    pairs = length // (2 * block)
    lanes = np.arange(length).reshape(2, pairs, block).transpose(1, 0, 2).reshape(-1)
    turn = np.arange(half) * (2.0 * math.pi / length)
    turn = np.stack([np.cos(turn), np.sin(turn)])
    down = np.broadcast_to(turn[:, :, None], (2, half, LANES)).astype(np.float32)
    across = np.broadcast_to(turn[:, None, :], (2, 8, half)).astype(np.float32)
    tables = split_table(rows), split_table(right[lanes]), split_table(right[:, lanes])
    return *tables, down, across


def swap_halves(packed):
    return pltpu.roll(packed, LANES // 2, axis=packed.ndim - 1)


def pack_pair(first, second, low_half):
    left = jnp.where(low_half, first, swap_halves(second))
    right = jnp.where(low_half, swap_halves(first), second)
    return left, right


def lane_order(back=False):
    row = lax.broadcasted_iota(jnp.int32, (LANES, LANES), 0)
    column = lax.broadcasted_iota(jnp.int32, (LANES, LANES), 1)
    plain, moved = (column, row) if back else (row, column)
    block = LANES // 2
    inner = moved % block
    source = moved - inner + 2 * (inner % (block // 2)) + inner // (block // 2)
    return jnp.where(plain == source, 1.0, 0.0).astype(jnp.bfloat16)


def move_lanes(values, order):
    total = None
    for _ in range(3):
        part = values.astype(jnp.bfloat16)
        values = values - part.astype(jnp.float32)
        moved = jnp.dot(part, order, preferred_element_type=jnp.float32)
        total = moved if total is None else total + moved
    return total


def low_lanes(rows):
    return lax.broadcasted_iota(jnp.int32, (rows, LANES), 1) < LANES // 2


def prep_kernel(place_ref, spectrum_ref, keep_ref, send_ref, pair_ref):
    rows, width = spectrum_ref.shape[1:]
    low_half = low_lanes(rows // 2)
    first_core = place_ref[CORE] == 0
    order = lane_order()
    for group in range(width // LANES):
        for part in range(2):
            rounded = spectrum_ref[part, :, pl.ds(group * LANES, LANES)].astype(jnp.bfloat16)
            pair_ref[group, part] = jnp.dot(rounded, order, preferred_element_type=jnp.float32)
        halves = []
        for half in range(2):
            chosen = pl.ds(half, rows // 2, stride=2)
            halves.append(pack_pair(pair_ref[group, 0, chosen], pair_ref[group, 1, chosen], low_half))
        for side in range(2):
            even, odd = halves[0][side], halves[1][side]
            block = 2 * group + side
            keep_ref[block] = jnp.where(first_core, even, odd).astype(jnp.bfloat16)
            send_ref[block] = jnp.where(first_core, odd, even).astype(jnp.bfloat16)


def join_kernel(place_ref, own_ref, other_ref, out_ref):
    core = place_ref[CORE]
    out_ref[core] = own_ref[...]
    out_ref[1 - core] = other_ref[...]


def band_kernel(place_ref, *refs):
    parts, out_ref = refs[:-1], refs[-1]
    for source, part_ref in enumerate(parts):
        out_ref[lax.rem(place_ref[COLUMN] + len(parts) - source, len(parts))] = part_ref[...]


def pupil_kernel(pupil_ref, same_ref, cross_ref, pair_ref):
    bands, _, rows = same_ref.shape[1:4]
    low_half = low_lanes(rows)
    order = lane_order()
    for group in range(pupil_ref.shape[2] // LANES):
        for part in range(2):
            chosen = pupil_ref[part, :, pl.ds(group * LANES, LANES)]
            pair_ref[group, part] = move_lanes(chosen, order)
        for half in range(2):
            for band in range(bands):
                chosen = pl.ds(band * 2 * rows + half, rows, stride=2)
                real, imag = pair_ref[group, 0, chosen], pair_ref[group, 1, chosen]
                left, right = pack_pair(real, real, low_half)
                same_ref[half, band, 2 * group] = left
                same_ref[half, band, 2 * group + 1] = right
                left, right = pack_pair(-imag, imag, low_half)
                cross_ref[half, band, 2 * group] = left
                cross_ref[half, band, 2 * group + 1] = right


def select_kernel(place_ref, starts_ref, *refs):
    near, outs, rows_ref = refs[:4], refs[4:12], refs[12]
    blocks = near[0].shape[2]
    for source in range(4):
        first = CORES * lax.rem(place_ref[NEAR] + 4 - source, 4)
        for part in range(near[0].shape[0]):
            rows_ref[pl.ds(first, CORES), pl.ds(part * blocks, blocks)] = near[source][part]
    span = outs[0].shape[1]
    for peer in range(len(outs)):
        for row in range(rows_ref.shape[0]):
            outs[peer][row] = rows_ref[row, pl.ds(starts_ref[peer, row], span)]


def table_dot(left, right):
    return jnp.dot(left, right, preferred_element_type=jnp.float32)


def rows_of(place_ref, source, side, row):
    even = place_ref[CORE] == side
    band = CORES * lax.rem(place_ref[HEIGHT] + HEIGHTS - source, HEIGHTS) + lax.rem(row, CORES)
    step = lax.rem(row // CORES + DEPTHS - place_ref[DEPTH], DEPTHS)
    return (
        jnp.where(even, (DEPTHS - source) % DEPTHS, step),
        jnp.where(even, 0, 1),
        jnp.where(even, row, band),
    )


def block_lanes(rows):
    return lax.broadcasted_iota(jnp.int32, (rows, LANES), 1) % (LANES // 2) < LANES // 4


def columns_in(place_ref, source, windows, same_ref, cross_ref, spread_ref, packed_ref, stacked_ref):
    bands, blocks, rows = windows[0].shape[:3]
    taken = bands * rows
    even_lanes = block_lanes(rows)
    for side in range(CORES):
        for row in range(bands):
            _, half, band = rows_of(place_ref, source, side, row)
            place = pl.ds(side * taken + row * rows, rows)
            for pair in range(blocks // 2):
                waves = []
                for block in (2 * pair, 2 * pair + 1):
                    window = windows[side][row, block]
                    wave = same_ref[half, band, block] * window.astype(jnp.float32)
                    wave += cross_ref[half, band, block] * swap_halves(window).astype(jnp.float32)
                    waves.append(wave.astype(jnp.bfloat16))
                lanes = pl.ds(pair * LANES, LANES)
                even = jnp.where(even_lanes, waves[0], pltpu.roll(waves[1], LANES // 4, 1))
                odd = jnp.where(even_lanes, pltpu.roll(waves[0], LANES - LANES // 4, 1), waves[1])
                packed_ref[0, place, lanes] = even
                packed_ref[1, place, lanes] = odd

    for parity in range(2):
        for part in range(2):
            lanes = pl.ds(part * taken, taken)
            product = table_dot(packed_ref[parity], spread_ref[0, :, lanes])
            product += table_dot(packed_ref[parity], spread_ref[1, :, lanes])
            product = product.astype(jnp.bfloat16)
            for side in range(CORES):
                for row in range(bands):
                    step, half, band = rows_of(place_ref, source, side, row)
                    place = pl.ds(pl.multiple_of(part * taken + band * rows, rows), rows)
                    start = side * taken + row * rows
                    stacked_ref[step, parity, half, place] = product[start:start + rows]


def columns_out(place_ref, source, outs, same_ref, cross_ref, gather_ref, spectral_ref, packed_ref):
    bands, blocks, rows = outs[0].shape[:3]
    taken = bands * rows
    even_lanes = block_lanes(rows)
    for side in range(CORES):
        for row in range(bands):
            step, half, band = rows_of(place_ref, source, side, row)
            place = pl.ds(pl.multiple_of(half * taken + band * rows, rows), rows)
            start = side * taken + row * rows
            for parity in range(2):
                packed_ref[parity, start:start + rows] = spectral_ref[step, parity, place]
    for tile in range(2):
        lanes = pl.ds(tile * TILE, TILE)
        products = []
        for parity in range(2):
            product = table_dot(packed_ref[parity], gather_ref[0, :, lanes])
            products.append(product + table_dot(packed_ref[parity], gather_ref[1, :, lanes]))
        for side in range(CORES):
            for row in range(bands):
                _, half, band = rows_of(place_ref, source, side, row)
                start = side * taken + row * rows
                for inner in range(TILE // LANES):
                    pair = tile * (TILE // LANES) + inner
                    even, odd = (
                        product[start:start + rows, inner * LANES:(inner + 1) * LANES]
                        for product in products
                    )
                    left = jnp.where(even_lanes, even, pltpu.roll(odd, LANES // 4, 1))
                    right = jnp.where(even_lanes, pltpu.roll(even, LANES - LANES // 4, 1), odd)
                    for block, spectral in ((2 * pair, left), (2 * pair + 1, right)):
                        update = same_ref[half, band, block] * spectral
                        update += cross_ref[half, band, block] * swap_halves(spectral)
                        outs[side][row, block] = update.astype(jnp.bfloat16)


def first_kernel(place_ref, *refs):
    count = len(EARLY)
    windows, (same_ref, cross_ref, spread_ref) = refs[:2 * count], refs[2 * count:2 * count + 3]
    stacked_ref, packed_ref = refs[2 * count + 3:]
    for index, source in enumerate(EARLY):
        columns_in(
            place_ref, source, windows[2 * index:2 * index + 2], same_ref, cross_ref, spread_ref,
            packed_ref, stacked_ref,
        )


def last_kernel(place_ref, spectral_ref, same_ref, cross_ref, gather_ref, *refs):
    outs, packed_ref = refs[:-1], refs[-1]
    for index, source in enumerate(LATE):
        columns_out(
            place_ref, source, outs[2 * index:2 * index + 2], same_ref, cross_ref, gather_ref,
            spectral_ref, packed_ref,
        )


def led_kernel(
    place_ref, leds_ref, early_ref, window0_ref, window1_ref, window2_ref, window3_ref, measured_ref,
    same_ref, cross_ref, rows_ref, spread_ref, gather_ref, down_ref, across_ref,
    update0_ref, update1_ref, update2_ref, update3_ref, spectral_ref, stacked_ref, packed_ref,
):
    steps = stacked_ref.shape[0]
    half_size = stacked_ref.shape[4]
    stacked_ref[...] = early_ref[...]
    windows = (window0_ref, window1_ref), (window2_ref, window3_ref)
    for source, pair in zip(LATE, windows):
        columns_in(place_ref, source, pair, same_ref, cross_ref, spread_ref, packed_ref, stacked_ref)

    turn_re = jnp.concatenate([down_ref[0]] * (half_size // LANES), axis=1)
    turn_im = jnp.concatenate([down_ref[1]] * (half_size // LANES), axis=1)
    down, across = (turn_re, turn_im), (across_ref[0, 0:1], across_ref[1, 0:1])

    def turned(pair, by):
        return pair[0] * by[0] - pair[1] * by[1], pair[0] * by[1] + pair[1] * by[0]

    def plus(left, right):
        return left[0] + right[0], left[1] + right[1]

    def minus(left, right):
        return left[0] - right[0], left[1] - right[1]

    @pl.loop(0, steps)
    def _(step):
        led = leds_ref[step]

        def row_transform(half, parity):
            moved = table_dot(rows_ref[0], stacked_ref[step, parity, half])
            moved += table_dot(rows_ref[1], stacked_ref[step, parity, half])
            return moved[:half_size], moved[half_size:]

        def residual(field, row, lane):
            measured = measured_ref[led, pl.ds(row, half_size), pl.ds(lane, half_size)]
            real, imag = field
            factor = 1.0 - measured * lax.rsqrt(real * real + imag * imag + floor_sq)
            return real * factor, -imag * factor

        tops, lows = [], []
        for parity in range(2):
            first = row_transform(0, parity)
            second = turned(row_transform(1, parity), down)
            tops.append(plus(first, second))
            lows.append(minus(first, second))
        parts = []
        for row, (first, second) in ((0, tops), (half_size, lows)):
            second = turned(second, across)
            left = residual(plus(first, second), row, 0)
            right = residual(minus(first, second), row, half_size)
            parts.append((plus(left, right), turned(minus(left, right), across)))
        for parity in range(2):
            top, low = parts[0][parity], parts[1][parity]
            for half, value in enumerate((plus(top, low), turned(minus(top, low), down))):
                for part in range(2):
                    stacked_ref[step, parity, half, pl.ds(part * half_size, half_size)] = value[
                        part
                    ].astype(jnp.bfloat16)
        for parity in range(2):
            for half in range(2):
                moved = row_transform(half, parity)
                for part in range(2):
                    spectral_ref[
                        step, parity, pl.ds(half * half_size, half_size), pl.ds(part * half_size, half_size)
                    ] = moved[part].astype(jnp.bfloat16)

    updates = (update0_ref, update1_ref), (update2_ref, update3_ref)
    for source, pair in zip(EARLY, updates):
        columns_out(place_ref, source, pair, same_ref, cross_ref, gather_ref, spectral_ref, packed_ref)


def collect_kernel(place_ref, starts_ref, *refs):
    updates, outs, total_ref = refs[:8], refs[8:12], refs[12]
    span = updates[0].shape[1]
    for peer in range(4):
        first = CORES * lax.rem(place_ref[NEAR] + peer, 4)
        for side in range(CORES):
            total_ref[...] = jnp.zeros_like(total_ref)
            for source in range(8):
                place = pl.ds(starts_ref[source, first + side], span)
                total_ref[place] = total_ref[place] + updates[source][first + side].astype(jnp.float32)
            outs[peer][side] = total_ref[...].astype(outs[peer].dtype)


def columns_kernel(place_ref, *refs):
    parts, outs = refs[:4], refs[4:]
    blocks = outs[0].shape[1]
    for peer in range(len(outs)):
        place = pl.ds(lax.rem(place_ref[COLUMN] + peer, len(outs)) * blocks, blocks)
        for side in range(CORES):
            total = parts[0][side, place].astype(jnp.float32)
            for part in parts[1:]:
                total = total + part[side, place].astype(jnp.float32)
            outs[peer][side] = total.astype(outs[peer].dtype)


def halves_kernel(place_ref, part0_ref, part1_ref, part2_ref, part3_ref, keep_ref, send_ref):
    core = place_ref[CORE]
    for out_ref, side in ((keep_ref, core), (send_ref, 1 - core)):
        total = part0_ref[side].astype(jnp.float32)
        for part_ref in (part1_ref, part2_ref, part3_ref):
            total = total + part_ref[side].astype(jnp.float32)
        out_ref[...] = total


def final_kernel(place_ref, own_ref, other_ref, spectrum_ref, out_ref, pair_ref):
    rows, width = spectrum_ref.shape[1:]
    low_half = low_lanes(rows // 2)
    first_core = place_ref[CORE] == 0
    back = lane_order(back=True)
    for group in range(width // LANES):
        for half in range(2):
            sums = []
            for block in (2 * group, 2 * group + 1):
                pair = (own_ref[block], other_ref[block])
                sums.append(jnp.where(first_core, pair[half], pair[1 - half]))
            real, imag = pack_pair(sums[0], sums[1], low_half)
            chosen = pl.ds(half, rows // 2, stride=2)
            pair_ref[group, 0, chosen] = -step_size * real
            pair_ref[group, 1, chosen] = step_size * imag
        lanes = pl.ds(group * LANES, LANES)
        for part in range(2):
            step = move_lanes(pair_ref[group, part], back)
            out_ref[part, :, lanes] = spectrum_ref[part, :, lanes] + step


def call(kernel, outs, inputs, mib, name, scalars=0, scratch=(), flops=0):
    size = sum(math.prod(out.shape) * out.dtype.itemsize for out in outs)
    size += sum(math.prod(array.shape) * array.dtype.itemsize for array in inputs)
    return pl.pallas_call(
        kernel,
        out_shape=tuple(outs),
        in_specs=[SMEM] * scalars + [VMEM] * (len(inputs) - scalars),
        out_specs=(VMEM,) * len(outs),
        scratch_shapes=list(scratch),
        compiler_params=params(mib),
        cost_estimate=pl.CostEstimate(flops=flops, bytes_accessed=size, transcendentals=0),
        name=name,
    )(*inputs)


TILES = DEPTHS * HEIGHTS * CORES


def tile_of(depth, height, core):
    return (depth % DEPTHS * HEIGHTS + height % HEIGHTS) * CORES + core


def tile_moves(even_move, odd_move):
    pairs = []
    for tile in range(TILES):
        depth, height, core = tile // (HEIGHTS * CORES), tile // CORES % HEIGHTS, tile % CORES
        pairs.append((tile, tile_of(*(odd_move if core else even_move)(depth, height))))
    return pairs


def far_moves(steps, side):
    return tile_moves(
        lambda depth, height: (depth + steps, height, side),
        lambda depth, height: (depth, height + steps, 1 - side),
    )


def near_moves(steps):
    return tile_moves(
        lambda depth, height: (depth, height + steps, 0),
        lambda depth, height: (depth + steps, height, 1),
    )


def reverse(moves):
    return [(target, source) for source, target in moves]


def send(array, moves, axis="tile"):
    return lax.ppermute(array, axis, moves)


def on_device(spectrum, pupil_field, amplitude, offsets):
    columns = lax.axis_size("col")
    tile, column = lax.axis_index("tile"), lax.axis_index("col")
    depth, height, core = tile // (HEIGHTS * CORES), tile // CORES % HEIGHTS, tile % CORES
    block_rows, own_width = spectrum.shape[1:]
    size = pupil_field.shape[1]
    span = size // block_rows
    own_blocks = own_width // block_rows
    band_blocks = own_blocks * columns
    rows = block_rows // 2
    bf16, f32 = jnp.bfloat16, jnp.float32
    shaped = lambda *shape, dtype=bf16: jax.ShapeDtypeStruct(shape, dtype)
    near = jnp.where(core == 0, height, depth)
    place = jnp.stack([depth, height, core, column, near]).astype(jnp.int32)
    swap = [(t, t ^ 1) for t in range(TILES)]

    wanted = jnp.arange(DEPTHS, dtype=jnp.int32) * span
    mine = offsets[None, :, 0] == wanted[:, None]
    slots = jnp.arange(offsets.shape[0], dtype=jnp.int32)[None]
    leds = jnp.roll(jnp.sum(jnp.where(mine, slots, 0), axis=1), -depth).astype(jnp.int32)
    firsts = jnp.sum(jnp.where(mine, offsets[None, :, 1], 0), axis=1).astype(jnp.int32)
    chip = jnp.stack([firsts, send(firsts, swap)])
    chips = jnp.stack([chip] + [send(chip, reverse(far_moves(steps, 0))) for steps in range(1, 4)])
    by_row = jnp.repeat(chips, CORES, axis=2)
    same_band = jnp.broadcast_to(lax.dynamic_slice_in_dim(chips, depth, 1, 2), by_row.shape)
    starts = jnp.where(core == 0, same_band, by_row).reshape(8, span).astype(jnp.int32)

    pairs = lambda width: [pltpu.VMEM((width // LANES, 2, block_rows, LANES), f32)]
    part_shape = (own_blocks, rows, LANES)
    tables = [jnp.asarray(table) for table in dft_tables(size, block_rows)]
    keep, give = call(
        prep_kernel,
        [shaped(*part_shape)] * 2,
        [place, spectrum],
        4,
        "prep",
        scalars=1,
        scratch=pairs(own_width),
    )
    joined, = call(
        join_kernel, [shaped(CORES, *part_shape)], [place, keep, send(give, swap)], 2, "join", scalars=1
    )
    along = lambda steps: [(c, (c + steps) % columns) for c in range(columns)]
    band, = call(
        band_kernel,
        [shaped(columns, CORES, *part_shape)],
        [place, joined] + [send(joined, along(steps), "col") for steps in range(1, columns)],
        4,
        "band",
        scalars=1,
    )
    near_parts = [band] + [send(band, near_moves(steps)) for steps in range(1, 4)]
    windows = call(
        select_kernel,
        [shaped(span, span, rows, LANES)] * 8,
        [place, starts] + near_parts,
        56,
        "select",
        scalars=2,
        scratch=[pltpu.VMEM((span, band_blocks, rows, LANES), bf16)],
    )
    far = [far_moves(steps, side) for steps in range(4) for side in range(CORES)]
    early = [2 * source + side for source in EARLY for side in range(CORES)]
    late = [2 * source + side for source in LATE for side in range(CORES)]
    incoming = [send(windows[peer], far[peer]) if peer else windows[0] for peer in early]
    late_windows = [send(windows[peer], far[peer]) for peer in late]

    pupil_field, incoming[1] = lax.optimization_barrier((pupil_field, incoming[1]))
    pupil_shape = shaped(2, span, span, rows, LANES, dtype=f32)
    same, cross = call(pupil_kernel, [pupil_shape] * 2, [pupil_field], 8, "pupil", scratch=[
        pltpu.VMEM((size // LANES, 2, size, LANES), f32)
    ])
    stacked_shape = (DEPTHS, 2, 2, size, size // 2)
    packed_scratch = pltpu.VMEM((2, size, size), bf16)
    window_shape = shaped(span, span, rows, LANES)
    rows_table, spread, gather, down, across = tables
    stacked, = call(
        first_kernel,
        [shaped(*stacked_shape)],
        [place, *incoming, same, cross, spread],
        12,
        "first",
        scalars=1,
        scratch=[packed_scratch],
        flops=48 * size**3,
    )
    *first_updates, spectral = call(
        led_kernel,
        [window_shape] * len(early) + [shaped(DEPTHS, 2, size, size)],
        [place, leds, stacked, *late_windows]
        + [amplitude, same, cross, rows_table, spread, gather, down, across],
        16,
        "leds",
        scalars=2,
        scratch=[pltpu.VMEM(stacked_shape, bf16), packed_scratch],
        flops=128 * size**3,
    )
    rest = call(
        last_kernel,
        [window_shape] * len(late),
        [place, spectral, same, cross, gather],
        12,
        "last",
        scalars=1,
        scratch=[packed_scratch],
        flops=48 * size**3,
    )
    returned = [None] * 8
    for peer, update in zip(early, first_updates):
        returned[peer] = send(update, reverse(far[peer])) if peer else update
    rest, returned[1] = lax.optimization_barrier((list(rest), returned[1]))
    for peer, update in zip(late, rest):
        returned[peer] = send(update, reverse(far[peer]))

    sum_shape = (CORES, band_blocks, rows, LANES)
    sums = call(
        collect_kernel,
        [shaped(*sum_shape, dtype=f32)] + [shaped(*sum_shape)] * 3,
        [place, starts] + returned,
        4,
        "collect",
        scalars=2,
        scratch=[pltpu.VMEM(sum_shape[1:], f32)],
    )
    near_sums = [sums[0]] + [send(sums[steps], near_moves(steps)) for steps in range(1, 4)]
    cut = call(
        columns_kernel,
        [shaped(CORES, *part_shape, dtype=f32)] + [shaped(CORES, *part_shape)] * (columns - 1),
        [place] + near_sums,
        4,
        "columns",
        scalars=1,
    )
    parts = [cut[0]] + [send(cut[steps], along(steps), "col") for steps in range(1, columns)]
    keep, give = call(
        halves_kernel, [shaped(*part_shape, dtype=f32)] * 2, [place] + parts, 2, "halves", scalars=1
    )
    return call(
        final_kernel,
        [shaped(*spectrum.shape, dtype=f32)],
        [place, keep, send(give, swap), spectrum],
        4,
        "final",
        scalars=1,
        scratch=pairs(own_width),
    )[0]


def solution(mesh):
    in_specs = (
        P(None, "tile", "col"),
        P(),
        P(("tile", "col"), None, None),
        P(("tile", "col"), None),
    )
    return jax.shard_map(
        on_device, mesh=mesh, in_specs=in_specs, out_specs=P(None, "tile", "col"), check_vma=False
    )
```

```python
import math

import jax
import jax.numpy as jnp
import numpy as np
from jax import lax
from jax.experimental import pallas as pl
from jax.experimental.pallas import tpu as pltpu
from jax.sharding import PartitionSpec as P

floor_sq = 0.25
step_size = 0.5
LANES = 128
DEPTHS, HEIGHTS, CORES = 4, 4, 2
TILE = 256
BACK_ORDER = 0, 4, 5, 1, 2, 6, 3, 7
EARLY, LATE = (2, 0), (1, 3)
DEPTH, HEIGHT, CORE, COLUMN, NEAR = range(5)
VMEM = pl.BlockSpec(memory_space=pltpu.VMEM)
SMEM = pl.BlockSpec(memory_space=pltpu.SMEM)


def params(mib, **more):
    return pltpu.CompilerParams(vmem_limit_bytes=mib * 2**20, **more)


def split_table(table):
    high = table.astype(jnp.bfloat16)
    low = (table - high.astype(np.float64)).astype(jnp.bfloat16)
    return np.stack([high, low])


def dft_tables(length, block):
    half = length // 2
    counter = np.arange(half)
    angles = (counter[:, None] * counter[None, :] % half) * (2.0 * math.pi / half)
    cosine = np.cos(angles) / math.sqrt(length)
    sine = np.sin(angles) / math.sqrt(length)
    rows = np.block([[cosine, -sine], [sine, cosine]])
    right = np.block([[cosine, sine], [-sine, cosine]])
    pairs = length // (2 * block)
    lanes = np.arange(length).reshape(2, pairs, block).transpose(1, 0, 2).reshape(-1)
    turn = np.arange(half) * (2.0 * math.pi / length)
    turn = np.stack([np.cos(turn), np.sin(turn)])
    down = np.broadcast_to(turn[:, :, None], (2, half, LANES)).astype(np.float32)
    across = np.broadcast_to(turn[:, None, :], (2, 8, half)).astype(np.float32)
    tables = split_table(rows), split_table(right[lanes]), split_table(right[:, lanes])
    return *tables, down, across


def swap_halves(packed):
    return pltpu.roll(packed, LANES // 2, axis=packed.ndim - 1)


def pack_pair(first, second, low_half):
    left = jnp.where(low_half, first, swap_halves(second))
    right = jnp.where(low_half, swap_halves(first), second)
    return left, right


def lane_order(back=False):
    row = lax.broadcasted_iota(jnp.int32, (LANES, LANES), 0)
    column = lax.broadcasted_iota(jnp.int32, (LANES, LANES), 1)
    plain, moved = (column, row) if back else (row, column)
    block = LANES // 2
    inner = moved % block
    source = moved - inner + 2 * (inner % (block // 2)) + inner // (block // 2)
    return jnp.where(plain == source, 1.0, 0.0).astype(jnp.bfloat16)


def move_lanes(values, order):
    total = None
    for _ in range(3):
        part = values.astype(jnp.bfloat16)
        values = values - part.astype(jnp.float32)
        moved = jnp.dot(part, order, preferred_element_type=jnp.float32)
        total = moved if total is None else total + moved
    return total


def low_lanes(rows):
    return lax.broadcasted_iota(jnp.int32, (rows, LANES), 1) < LANES // 2


def prep_kernel(place_ref, spectrum_ref, keep_ref, send_ref, pair_ref):
    rows, width = spectrum_ref.shape[1:]
    low_half = low_lanes(rows // 2)
    first_core = place_ref[CORE] == 0
    order = lane_order()
    for group in range(width // LANES):
        for part in range(2):
            rounded = spectrum_ref[part, :, pl.ds(group * LANES, LANES)].astype(jnp.bfloat16)
            pair_ref[group, part] = jnp.dot(rounded, order, preferred_element_type=jnp.float32)
        halves = []
        for half in range(2):
            chosen = pl.ds(half, rows // 2, stride=2)
            halves.append(pack_pair(pair_ref[group, 0, chosen], pair_ref[group, 1, chosen], low_half))
        for side in range(2):
            even, odd = halves[0][side], halves[1][side]
            block = 2 * group + side
            keep_ref[block] = jnp.where(first_core, even, odd).astype(jnp.bfloat16)
            send_ref[block] = jnp.where(first_core, odd, even).astype(jnp.bfloat16)


def join_kernel(place_ref, own_ref, other_ref, out_ref):
    core = place_ref[CORE]
    out_ref[core] = own_ref[...]
    out_ref[1 - core] = other_ref[...]


def band_kernel(place_ref, *refs):
    parts, out_ref = refs[:-1], refs[-1]
    for source, part_ref in enumerate(parts):
        out_ref[lax.rem(place_ref[COLUMN] + len(parts) - source, len(parts))] = part_ref[...]


def pupil_kernel(pupil_ref, same_ref, cross_ref, pair_ref):
    bands, _, rows = same_ref.shape[1:4]
    low_half = low_lanes(rows)
    order = lane_order()
    for group in range(pupil_ref.shape[2] // LANES):
        for part in range(2):
            chosen = pupil_ref[part, :, pl.ds(group * LANES, LANES)]
            pair_ref[group, part] = move_lanes(chosen, order)
        for half in range(2):
            for band in range(bands):
                chosen = pl.ds(band * 2 * rows + half, rows, stride=2)
                real, imag = pair_ref[group, 0, chosen], pair_ref[group, 1, chosen]
                left, right = pack_pair(real, real, low_half)
                same_ref[half, band, 2 * group] = left
                same_ref[half, band, 2 * group + 1] = right
                left, right = pack_pair(-imag, imag, low_half)
                cross_ref[half, band, 2 * group] = left
                cross_ref[half, band, 2 * group + 1] = right


def select_kernel(place_ref, starts_ref, *refs):
    near, outs, rows_ref = refs[:4], refs[4:12], refs[12]
    blocks = near[0].shape[2]
    for source in range(4):
        first = CORES * lax.rem(place_ref[NEAR] + 4 - source, 4)
        for part in range(near[0].shape[0]):
            rows_ref[pl.ds(first, CORES), pl.ds(part * blocks, blocks)] = near[source][part]
    span = outs[0].shape[1]
    for peer in range(len(outs)):
        for row in range(rows_ref.shape[0]):
            outs[peer][row] = rows_ref[row, pl.ds(starts_ref[peer, row], span)]


def table_dot(left, right):
    return jnp.dot(left, right, preferred_element_type=jnp.float32)


def rows_of(place_ref, source, side, row):
    even = place_ref[CORE] == side
    band = CORES * lax.rem(place_ref[HEIGHT] + HEIGHTS - source, HEIGHTS) + lax.rem(row, CORES)
    step = lax.rem(row // CORES + DEPTHS - place_ref[DEPTH], DEPTHS)
    return (
        jnp.where(even, (DEPTHS - source) % DEPTHS, step),
        jnp.where(even, 0, 1),
        jnp.where(even, row, band),
    )


def block_lanes(rows):
    return lax.broadcasted_iota(jnp.int32, (rows, LANES), 1) % (LANES // 2) < LANES // 4


def columns_in(place_ref, source, windows, same_ref, cross_ref, spread_ref, packed_ref, stacked_ref):
    bands, blocks, rows = windows[0].shape[:3]
    taken = bands * rows
    even_lanes = block_lanes(rows)
    for side in range(CORES):
        for row in range(bands):
            _, half, band = rows_of(place_ref, source, side, row)
            place = pl.ds(side * taken + row * rows, rows)
            for pair in range(blocks // 2):
                waves = []
                for block in (2 * pair, 2 * pair + 1):
                    window = windows[side][row, block]
                    wave = same_ref[half, band, block] * window.astype(jnp.float32)
                    wave += cross_ref[half, band, block] * swap_halves(window).astype(jnp.float32)
                    waves.append(wave.astype(jnp.bfloat16))
                lanes = pl.ds(pair * LANES, LANES)
                even = jnp.where(even_lanes, waves[0], pltpu.roll(waves[1], LANES // 4, 1))
                odd = jnp.where(even_lanes, pltpu.roll(waves[0], LANES - LANES // 4, 1), waves[1])
                packed_ref[0, place, lanes] = even
                packed_ref[1, place, lanes] = odd

    for parity in range(2):
        for part in range(2):
            lanes = pl.ds(part * taken, taken)
            product = table_dot(packed_ref[parity], spread_ref[0, :, lanes])
            product += table_dot(packed_ref[parity], spread_ref[1, :, lanes])
            product = product.astype(jnp.bfloat16)
            for side in range(CORES):
                for row in range(bands):
                    step, half, band = rows_of(place_ref, source, side, row)
                    place = pl.ds(pl.multiple_of(part * taken + band * rows, rows), rows)
                    start = side * taken + row * rows
                    stacked_ref[step, parity, half, place] = product[start:start + rows]


def columns_out(place_ref, source, outs, same_ref, cross_ref, gather_ref, spectral_ref, packed_ref):
    bands, blocks, rows = outs[0].shape[:3]
    taken = bands * rows
    even_lanes = block_lanes(rows)
    for side in range(CORES):
        for row in range(bands):
            step, half, band = rows_of(place_ref, source, side, row)
            place = pl.ds(pl.multiple_of(half * taken + band * rows, rows), rows)
            start = side * taken + row * rows
            for parity in range(2):
                packed_ref[parity, start:start + rows] = spectral_ref[step, parity, place]
    for tile in range(2):
        lanes = pl.ds(tile * TILE, TILE)
        products = []
        for parity in range(2):
            product = table_dot(packed_ref[parity], gather_ref[0, :, lanes])
            products.append(product + table_dot(packed_ref[parity], gather_ref[1, :, lanes]))
        for side in range(CORES):
            for row in range(bands):
                _, half, band = rows_of(place_ref, source, side, row)
                start = side * taken + row * rows
                for inner in range(TILE // LANES):
                    pair = tile * (TILE // LANES) + inner
                    even, odd = (
                        product[start:start + rows, inner * LANES:(inner + 1) * LANES]
                        for product in products
                    )
                    left = jnp.where(even_lanes, even, pltpu.roll(odd, LANES // 4, 1))
                    right = jnp.where(even_lanes, pltpu.roll(even, LANES - LANES // 4, 1), odd)
                    for block, spectral in ((2 * pair, left), (2 * pair + 1, right)):
                        update = same_ref[half, band, block] * spectral
                        update += cross_ref[half, band, block] * swap_halves(spectral)
                        outs[side][row, block] = update.astype(jnp.bfloat16)


def first_kernel(place_ref, *refs):
    count = len(EARLY)
    windows, (same_ref, cross_ref, spread_ref) = refs[:2 * count], refs[2 * count:2 * count + 3]
    stacked_ref, packed_ref = refs[2 * count + 3:]
    for index, source in enumerate(EARLY):
        columns_in(
            place_ref, source, windows[2 * index:2 * index + 2], same_ref, cross_ref, spread_ref,
            packed_ref, stacked_ref,
        )


def last_kernel(place_ref, spectral_ref, same_ref, cross_ref, gather_ref, *refs):
    outs, packed_ref = refs[:-1], refs[-1]
    for index, source in enumerate(LATE):
        columns_out(
            place_ref, source, outs[index::len(LATE)], same_ref, cross_ref, gather_ref,
            spectral_ref, packed_ref,
        )


def led_kernel(
    place_ref, leds_ref, early_ref, window0_ref, window1_ref, window2_ref, window3_ref, measured_ref,
    same_ref, cross_ref, rows_ref, spread_ref, gather_ref, down_ref, across_ref,
    update0_ref, update1_ref, update2_ref, update3_ref, spectral_ref, stacked_ref, packed_ref,
):
    steps = stacked_ref.shape[0]
    half_size = stacked_ref.shape[4]
    stacked_ref[...] = early_ref[...]
    windows = (window0_ref, window2_ref), (window1_ref, window3_ref)
    for source, pair in zip(LATE, windows):
        columns_in(place_ref, source, pair, same_ref, cross_ref, spread_ref, packed_ref, stacked_ref)

    turn_re = jnp.concatenate([down_ref[0]] * (half_size // LANES), axis=1)
    turn_im = jnp.concatenate([down_ref[1]] * (half_size // LANES), axis=1)
    down, across = (turn_re, turn_im), (across_ref[0, 0:1], across_ref[1, 0:1])

    def turned(pair, by):
        return pair[0] * by[0] - pair[1] * by[1], pair[0] * by[1] + pair[1] * by[0]

    def plus(left, right):
        return left[0] + right[0], left[1] + right[1]

    def minus(left, right):
        return left[0] - right[0], left[1] - right[1]

    @pl.loop(0, steps)
    def _(step):
        led = leds_ref[step]

        def row_transform(half, parity):
            moved = table_dot(rows_ref[0], stacked_ref[step, parity, half])
            moved += table_dot(rows_ref[1], stacked_ref[step, parity, half])
            return moved[:half_size], moved[half_size:]

        def residual(field, row, lane):
            measured = measured_ref[led, pl.ds(row, half_size), pl.ds(lane, half_size)]
            real, imag = field
            factor = 1.0 - measured * lax.rsqrt(real * real + imag * imag + floor_sq)
            return real * factor, -imag * factor

        tops, lows = [], []
        for parity in range(2):
            first = row_transform(0, parity)
            second = turned(row_transform(1, parity), down)
            tops.append(plus(first, second))
            lows.append(minus(first, second))
        parts = []
        for row, (first, second) in ((0, tops), (half_size, lows)):
            second = turned(second, across)
            left = residual(plus(first, second), row, 0)
            right = residual(minus(first, second), row, half_size)
            parts.append((plus(left, right), turned(minus(left, right), across)))
        for parity in range(2):
            top, low = parts[0][parity], parts[1][parity]
            for half, value in enumerate((plus(top, low), turned(minus(top, low), down))):
                for part in range(2):
                    stacked_ref[step, parity, half, pl.ds(part * half_size, half_size)] = value[
                        part
                    ].astype(jnp.bfloat16)
        for parity in range(2):
            for half in range(2):
                moved = row_transform(half, parity)
                for part in range(2):
                    spectral_ref[
                        step, parity, pl.ds(half * half_size, half_size), pl.ds(part * half_size, half_size)
                    ] = moved[part].astype(jnp.bfloat16)

    updates = (update0_ref, update1_ref), (update2_ref, update3_ref)
    for source, pair in zip(EARLY, updates):
        columns_out(place_ref, source, pair, same_ref, cross_ref, gather_ref, spectral_ref, packed_ref)


def collect_kernel(place_ref, starts_ref, *refs):
    updates, outs, total_ref = [refs[BACK_ORDER.index(peer)] for peer in range(8)], refs[8:12], refs[12]
    span = updates[0].shape[1]
    for peer in range(4):
        first = CORES * lax.rem(place_ref[NEAR] + peer, 4)
        for side in range(CORES):
            total_ref[...] = jnp.zeros_like(total_ref)
            for source in range(8):
                place = pl.ds(starts_ref[source, first + side], span)
                total_ref[place] = total_ref[place] + updates[source][first + side].astype(jnp.float32)
            outs[peer][side] = total_ref[...].astype(outs[peer].dtype)


def columns_kernel(place_ref, *refs):
    parts, outs = refs[:4], refs[4:]
    blocks = outs[0].shape[1]
    for peer in range(len(outs)):
        place = pl.ds(lax.rem(place_ref[COLUMN] + peer, len(outs)) * blocks, blocks)
        for side in range(CORES):
            total = parts[0][side, place].astype(jnp.float32)
            for part in parts[1:]:
                total = total + part[side, place].astype(jnp.float32)
            outs[peer][side] = total.astype(outs[peer].dtype)


def halves_kernel(place_ref, part0_ref, part1_ref, part2_ref, part3_ref, keep_ref, send_ref):
    core = place_ref[CORE]
    for out_ref, side in ((keep_ref, core), (send_ref, 1 - core)):
        total = part0_ref[side].astype(jnp.float32)
        for part_ref in (part1_ref, part2_ref, part3_ref):
            total = total + part_ref[side].astype(jnp.float32)
        out_ref[...] = total


def final_kernel(place_ref, own_ref, other_ref, spectrum_ref, out_ref, pair_ref):
    rows, width = spectrum_ref.shape[1:]
    low_half = low_lanes(rows // 2)
    first_core = place_ref[CORE] == 0
    back = lane_order(back=True)
    for group in range(width // LANES):
        for half in range(2):
            sums = []
            for block in (2 * group, 2 * group + 1):
                pair = (own_ref[block], other_ref[block])
                sums.append(jnp.where(first_core, pair[half], pair[1 - half]))
            real, imag = pack_pair(sums[0], sums[1], low_half)
            chosen = pl.ds(half, rows // 2, stride=2)
            pair_ref[group, 0, chosen] = -step_size * real
            pair_ref[group, 1, chosen] = step_size * imag
        lanes = pl.ds(group * LANES, LANES)
        for part in range(2):
            step = move_lanes(pair_ref[group, part], back)
            out_ref[part, :, lanes] = spectrum_ref[part, :, lanes] + step


def call(kernel, outs, inputs, mib, name, scalars=0, scratch=(), flops=0):
    size = sum(math.prod(out.shape) * out.dtype.itemsize for out in outs)
    size += sum(math.prod(array.shape) * array.dtype.itemsize for array in inputs)
    return pl.pallas_call(
        kernel,
        out_shape=tuple(outs),
        in_specs=[SMEM] * scalars + [VMEM] * (len(inputs) - scalars),
        out_specs=(VMEM,) * len(outs),
        scratch_shapes=list(scratch),
        compiler_params=params(mib),
        cost_estimate=pl.CostEstimate(flops=flops, bytes_accessed=size, transcendentals=0),
        name=name,
    )(*inputs)


TILES = DEPTHS * HEIGHTS * CORES


def tile_of(depth, height, core):
    return (depth % DEPTHS * HEIGHTS + height % HEIGHTS) * CORES + core


def tile_moves(even_move, odd_move):
    pairs = []
    for tile in range(TILES):
        depth, height, core = tile // (HEIGHTS * CORES), tile // CORES % HEIGHTS, tile % CORES
        pairs.append((tile, tile_of(*(odd_move if core else even_move)(depth, height))))
    return pairs


def far_moves(steps, side):
    return tile_moves(
        lambda depth, height: (depth + steps, height, side),
        lambda depth, height: (depth, height + steps, 1 - side),
    )


def near_moves(steps):
    return tile_moves(
        lambda depth, height: (depth, height + steps, 0),
        lambda depth, height: (depth + steps, height, 1),
    )


def reverse(moves):
    return [(target, source) for source, target in moves]


def send(array, moves, axis="tile"):
    return lax.ppermute(array, axis, moves)


def on_device(spectrum, pupil_field, amplitude, offsets):
    columns = lax.axis_size("col")
    tile, column = lax.axis_index("tile"), lax.axis_index("col")
    depth, height, core = tile // (HEIGHTS * CORES), tile // CORES % HEIGHTS, tile % CORES
    block_rows, own_width = spectrum.shape[1:]
    size = pupil_field.shape[1]
    span = size // block_rows
    own_blocks = own_width // block_rows
    band_blocks = own_blocks * columns
    rows = block_rows // 2
    bf16, f32 = jnp.bfloat16, jnp.float32
    shaped = lambda *shape, dtype=bf16: jax.ShapeDtypeStruct(shape, dtype)
    near = jnp.where(core == 0, height, depth)
    place = jnp.stack([depth, height, core, column, near]).astype(jnp.int32)
    swap = [(t, t ^ 1) for t in range(TILES)]

    wanted = jnp.arange(DEPTHS, dtype=jnp.int32) * span
    mine = offsets[None, :, 0] == wanted[:, None]
    slots = jnp.arange(offsets.shape[0], dtype=jnp.int32)[None]
    leds = jnp.roll(jnp.sum(jnp.where(mine, slots, 0), axis=1), -depth).astype(jnp.int32)
    firsts = jnp.sum(jnp.where(mine, offsets[None, :, 1], 0), axis=1).astype(jnp.int32)
    chip = jnp.stack([firsts, send(firsts, swap)])
    chips = jnp.stack([chip] + [send(chip, reverse(far_moves(steps, 0))) for steps in range(1, 4)])
    by_row = jnp.repeat(chips, CORES, axis=2)
    same_band = jnp.broadcast_to(lax.dynamic_slice_in_dim(chips, depth, 1, 2), by_row.shape)
    starts = jnp.where(core == 0, same_band, by_row).reshape(8, span).astype(jnp.int32)

    pairs = lambda width: [pltpu.VMEM((width // LANES, 2, block_rows, LANES), f32)]
    part_shape = (own_blocks, rows, LANES)
    tables = [jnp.asarray(table) for table in dft_tables(size, block_rows)]
    keep, give = call(
        prep_kernel,
        [shaped(*part_shape)] * 2,
        [place, spectrum],
        4,
        "prep",
        scalars=1,
        scratch=pairs(own_width),
    )
    joined, = call(
        join_kernel, [shaped(CORES, *part_shape)], [place, keep, send(give, swap)], 2, "join", scalars=1
    )
    along = lambda steps: [(c, (c + steps) % columns) for c in range(columns)]
    band, = call(
        band_kernel,
        [shaped(columns, CORES, *part_shape)],
        [place, joined] + [send(joined, along(steps), "col") for steps in range(1, columns)],
        4,
        "band",
        scalars=1,
    )
    near_parts = [band] + [send(band, near_moves(steps)) for steps in range(1, 4)]
    windows = call(
        select_kernel,
        [shaped(span, span, rows, LANES)] * 8,
        [place, starts] + near_parts,
        56,
        "select",
        scalars=2,
        scratch=[pltpu.VMEM((span, band_blocks, rows, LANES), bf16)],
    )
    far = [far_moves(steps, side) for steps in range(4) for side in range(CORES)]
    early = [2 * source + side for source in EARLY for side in range(CORES)]
    late = [2 * source + side for side in range(CORES) for source in LATE]
    incoming = [send(windows[peer], far[peer]) if peer else windows[0] for peer in early]
    late_windows = [send(windows[peer], far[peer]) for peer in late]

    pupil_field, incoming[1] = lax.optimization_barrier((pupil_field, incoming[1]))
    pupil_shape = shaped(2, span, span, rows, LANES, dtype=f32)
    same, cross = call(pupil_kernel, [pupil_shape] * 2, [pupil_field], 8, "pupil", scratch=[
        pltpu.VMEM((size // LANES, 2, size, LANES), f32)
    ])
    stacked_shape = (DEPTHS, 2, 2, size, size // 2)
    packed_scratch = pltpu.VMEM((2, size, size), bf16)
    window_shape = shaped(span, span, rows, LANES)
    rows_table, spread, gather, down, across = tables
    stacked, = call(
        first_kernel,
        [shaped(*stacked_shape)],
        [place, *incoming, same, cross, spread],
        12,
        "first",
        scalars=1,
        scratch=[packed_scratch],
        flops=48 * size**3,
    )
    *first_updates, spectral = call(
        led_kernel,
        [window_shape] * len(early) + [shaped(DEPTHS, 2, size, size)],
        [place, leds, stacked, *late_windows]
        + [amplitude, same, cross, rows_table, spread, gather, down, across],
        16,
        "leds",
        scalars=2,
        scratch=[pltpu.VMEM(stacked_shape, bf16), packed_scratch],
        flops=128 * size**3,
    )
    rest = call(
        last_kernel,
        [window_shape] * len(late),
        [place, spectral, same, cross, gather],
        12,
        "last",
        scalars=1,
        scratch=[packed_scratch],
        flops=48 * size**3,
    )
    returned = [None] * 8
    for peer, update in zip(early, first_updates):
        returned[peer] = send(update, reverse(far[peer])) if peer else update
    rest, returned[1] = lax.optimization_barrier((list(rest), returned[1]))
    for peer, update in zip(late, rest):
        returned[peer] = send(update, reverse(far[peer]))

    sum_shape = (CORES, band_blocks, rows, LANES)
    sums = call(
        collect_kernel,
        [shaped(*sum_shape, dtype=f32)] + [shaped(*sum_shape)] * 3,
        [place, starts] + [returned[peer] for peer in BACK_ORDER],
        4,
        "collect",
        scalars=2,
        scratch=[pltpu.VMEM(sum_shape[1:], f32)],
    )
    near_sums = [sums[0]] + [send(sums[steps], near_moves(steps)) for steps in range(1, 4)]
    cut = call(
        columns_kernel,
        [shaped(CORES, *part_shape, dtype=f32)] + [shaped(CORES, *part_shape)] * (columns - 1),
        [place] + near_sums,
        4,
        "columns",
        scalars=1,
    )
    parts = [cut[0]] + [send(cut[steps], along(steps), "col") for steps in range(1, columns)]
    keep, give = call(
        halves_kernel, [shaped(*part_shape, dtype=f32)] * 2, [place] + parts, 2, "halves", scalars=1
    )
    return call(
        final_kernel,
        [shaped(*spectrum.shape, dtype=f32)],
        [place, keep, send(give, swap), spectrum],
        4,
        "final",
        scalars=1,
        scratch=pairs(own_width),
    )[0]


def solution(mesh):
    in_specs = (
        P(None, "tile", "col"),
        P(),
        P(("tile", "col"), None, None),
        P(("tile", "col"), None),
    )
    return jax.shard_map(
        on_device, mesh=mesh, in_specs=in_specs, out_specs=P(None, "tile", "col"), check_vma=False
    )
```

```python
import functools
import math

import jax
import jax.numpy as jnp
import numpy as np
from jax import lax
from jax.experimental import pallas as pl
from jax.experimental.pallas import tpu as pltpu
from jax.sharding import PartitionSpec as P

floor_sq = 0.25
step_size = 0.5
LANES = 128
DEPTHS, HEIGHTS, CORES = 4, 4, 2
TILE = 256
BACK_ORDER = 0, 4, 5, 1, 2, 6, 3, 7
EARLY, LATE = (2, 0), (1, 3)
DEPTH, HEIGHT, CORE, COLUMN, NEAR = range(5)
VMEM = pl.BlockSpec(memory_space=pltpu.VMEM)
SMEM = pl.BlockSpec(memory_space=pltpu.SMEM)


def params(mib, **more):
    return pltpu.CompilerParams(vmem_limit_bytes=mib * 2**20, **more)


def split_table(table):
    high = table.astype(jnp.bfloat16)
    low = (table - high.astype(np.float64)).astype(jnp.bfloat16)
    return np.stack([high, low])


def dft_tables(length, block):
    half = length // 2
    counter = np.arange(half)
    angles = (counter[:, None] * counter[None, :] % half) * (2.0 * math.pi / half)
    cosine = np.cos(angles) / math.sqrt(length)
    sine = np.sin(angles) / math.sqrt(length)
    rows = np.block([[cosine, -sine], [sine, cosine]])
    right = np.block([[cosine, sine], [-sine, cosine]])
    pairs = length // (2 * block)
    lanes = np.arange(length).reshape(2, pairs, block).transpose(1, 0, 2).reshape(-1)
    turn = np.arange(half) * (2.0 * math.pi / length)
    turn = np.stack([np.cos(turn), np.sin(turn)])
    down = np.broadcast_to(turn[:, :, None], (2, half, LANES)).astype(np.float32)
    across = np.broadcast_to(turn[:, None, :], (2, 8, half)).astype(np.float32)
    tables = split_table(rows), split_table(right[lanes]), split_table(right[:, lanes])
    return *tables, down, across


def swap_halves(packed):
    return pltpu.roll(packed, LANES // 2, axis=packed.ndim - 1)


def pack_pair(first, second, low_half):
    left = jnp.where(low_half, first, swap_halves(second))
    right = jnp.where(low_half, swap_halves(first), second)
    return left, right


def lane_order(back=False):
    row = lax.broadcasted_iota(jnp.int32, (LANES, LANES), 0)
    column = lax.broadcasted_iota(jnp.int32, (LANES, LANES), 1)
    plain, moved = (column, row) if back else (row, column)
    block = LANES // 2
    inner = moved % block
    source = moved - inner + 2 * (inner % (block // 2)) + inner // (block // 2)
    return jnp.where(plain == source, 1.0, 0.0).astype(jnp.bfloat16)


def move_lanes(values, order):
    total = None
    for _ in range(3):
        part = values.astype(jnp.bfloat16)
        values = values - part.astype(jnp.float32)
        moved = jnp.dot(part, order, preferred_element_type=jnp.float32)
        total = moved if total is None else total + moved
    return total


def low_lanes(rows):
    return lax.broadcasted_iota(jnp.int32, (rows, LANES), 1) < LANES // 2


def prep_kernel(place_ref, spectrum_ref, keep_ref, send_ref, pair_ref):
    rows, width = spectrum_ref.shape[1:]
    low_half = low_lanes(rows // 2)
    first_core = place_ref[CORE] == 0
    order = lane_order()
    for group in range(width // LANES):
        for part in range(2):
            rounded = spectrum_ref[part, :, pl.ds(group * LANES, LANES)].astype(jnp.bfloat16)
            pair_ref[group, part] = jnp.dot(rounded, order, preferred_element_type=jnp.float32)
        halves = []
        for half in range(2):
            chosen = pl.ds(half, rows // 2, stride=2)
            halves.append(pack_pair(pair_ref[group, 0, chosen], pair_ref[group, 1, chosen], low_half))
        for side in range(2):
            even, odd = halves[0][side], halves[1][side]
            block = 2 * group + side
            keep_ref[block] = jnp.where(first_core, even, odd).astype(jnp.bfloat16)
            send_ref[block] = jnp.where(first_core, odd, even).astype(jnp.bfloat16)


def join_kernel(place_ref, own_ref, other_ref, out_ref):
    core = place_ref[CORE]
    out_ref[core] = own_ref[...]
    out_ref[1 - core] = other_ref[...]


def band_kernel(place_ref, *refs):
    parts, out_ref = refs[:-1], refs[-1]
    for source, part_ref in enumerate(parts):
        out_ref[lax.rem(place_ref[COLUMN] + len(parts) - source, len(parts))] = part_ref[...]


def pupil_kernel(pupil_ref, same_ref, cross_ref, pair_ref):
    bands, _, rows = same_ref.shape[1:4]
    low_half = low_lanes(rows)
    order = lane_order()
    for group in range(pupil_ref.shape[2] // LANES):
        for part in range(2):
            chosen = pupil_ref[part, :, pl.ds(group * LANES, LANES)]
            pair_ref[group, part] = move_lanes(chosen, order)
        for half in range(2):
            for band in range(bands):
                chosen = pl.ds(band * 2 * rows + half, rows, stride=2)
                real, imag = pair_ref[group, 0, chosen], pair_ref[group, 1, chosen]
                left, right = pack_pair(real, real, low_half)
                same_ref[half, band, 2 * group] = left
                same_ref[half, band, 2 * group + 1] = right
                left, right = pack_pair(-imag, imag, low_half)
                cross_ref[half, band, 2 * group] = left
                cross_ref[half, band, 2 * group + 1] = right


def select_kernel(place_ref, starts_ref, *refs):
    near, outs, rows_ref = refs[:4], refs[4:12], refs[12]
    blocks = near[0].shape[2]
    for source in range(4):
        first = CORES * lax.rem(place_ref[NEAR] + 4 - source, 4)
        for part in range(near[0].shape[0]):
            rows_ref[pl.ds(first, CORES), pl.ds(part * blocks, blocks)] = near[source][part]
    span = outs[0].shape[1]
    for peer in range(len(outs)):
        for row in range(rows_ref.shape[0]):
            outs[peer][row] = rows_ref[row, pl.ds(starts_ref[peer, row], span)]


def table_dot(left, right):
    return jnp.dot(left, right, preferred_element_type=jnp.float32)


def rows_of(place_ref, source, side, row):
    even = place_ref[CORE] == side
    band = CORES * lax.rem(place_ref[HEIGHT] + HEIGHTS - source, HEIGHTS) + lax.rem(row, CORES)
    step = lax.rem(row // CORES + DEPTHS - place_ref[DEPTH], DEPTHS)
    return (
        jnp.where(even, (DEPTHS - source) % DEPTHS, step),
        jnp.where(even, 0, 1),
        jnp.where(even, row, band),
    )


def block_lanes(rows):
    return lax.broadcasted_iota(jnp.int32, (rows, LANES), 1) % (LANES // 2) < LANES // 4


def columns_in(place_ref, source, windows, same_ref, cross_ref, spread_ref, packed_ref, stacked_ref):
    bands, blocks, rows = windows[0].shape[:3]
    taken = bands * rows
    even_lanes = block_lanes(rows)
    for side in range(CORES):
        for row in range(bands):
            _, half, band = rows_of(place_ref, source, side, row)
            place = pl.ds(side * taken + row * rows, rows)
            for pair in range(blocks // 2):
                waves = []
                for block in (2 * pair, 2 * pair + 1):
                    window = windows[side][row, block]
                    wave = same_ref[half, band, block] * window.astype(jnp.float32)
                    wave += cross_ref[half, band, block] * swap_halves(window).astype(jnp.float32)
                    waves.append(wave.astype(jnp.bfloat16))
                lanes = pl.ds(pair * LANES, LANES)
                even = jnp.where(even_lanes, waves[0], pltpu.roll(waves[1], LANES // 4, 1))
                odd = jnp.where(even_lanes, pltpu.roll(waves[0], LANES - LANES // 4, 1), waves[1])
                packed_ref[0, place, lanes] = even
                packed_ref[1, place, lanes] = odd

    for parity in range(2):
        for part in range(2):
            lanes = pl.ds(part * taken, taken)
            product = table_dot(packed_ref[parity], spread_ref[0, :, lanes])
            product += table_dot(packed_ref[parity], spread_ref[1, :, lanes])
            product = product.astype(jnp.bfloat16)
            for side in range(CORES):
                for row in range(bands):
                    step, half, band = rows_of(place_ref, source, side, row)
                    place = pl.ds(pl.multiple_of(part * taken + band * rows, rows), rows)
                    start = side * taken + row * rows
                    stacked_ref[step, parity, half, place] = product[start:start + rows]


def columns_out(place_ref, source, outs, same_ref, cross_ref, gather_ref, spectral_ref, packed_ref):
    bands, blocks, rows = outs[0].shape[:3]
    taken = bands * rows
    even_lanes = block_lanes(rows)
    for side in range(CORES):
        for row in range(bands):
            step, half, band = rows_of(place_ref, source, side, row)
            place = pl.ds(pl.multiple_of(half * taken + band * rows, rows), rows)
            start = side * taken + row * rows
            for parity in range(2):
                packed_ref[parity, start:start + rows] = spectral_ref[step, parity, place]
    for tile in range(2):
        lanes = pl.ds(tile * TILE, TILE)
        products = []
        for parity in range(2):
            product = table_dot(packed_ref[parity], gather_ref[0, :, lanes])
            products.append(product + table_dot(packed_ref[parity], gather_ref[1, :, lanes]))
        for side in range(CORES):
            for row in range(bands):
                _, half, band = rows_of(place_ref, source, side, row)
                start = side * taken + row * rows
                for inner in range(TILE // LANES):
                    pair = tile * (TILE // LANES) + inner
                    even, odd = (
                        product[start:start + rows, inner * LANES:(inner + 1) * LANES]
                        for product in products
                    )
                    left = jnp.where(even_lanes, even, pltpu.roll(odd, LANES // 4, 1))
                    right = jnp.where(even_lanes, pltpu.roll(even, LANES - LANES // 4, 1), odd)
                    for block, spectral in ((2 * pair, left), (2 * pair + 1, right)):
                        update = same_ref[half, band, block] * spectral
                        update += cross_ref[half, band, block] * swap_halves(spectral)
                        outs[side][row, block] = update.astype(jnp.bfloat16)


def first_kernel(place_ref, *refs):
    count = len(EARLY)
    windows, (same_ref, cross_ref, spread_ref) = refs[:2 * count], refs[2 * count:2 * count + 3]
    stacked_ref, packed_ref = refs[2 * count + 3:]
    for index, source in enumerate(EARLY):
        columns_in(
            place_ref, source, windows[2 * index:2 * index + 2], same_ref, cross_ref, spread_ref,
            packed_ref, stacked_ref,
        )


def last_kernel(place_ref, spectral_ref, same_ref, cross_ref, gather_ref, *refs):
    outs, packed_ref = refs[:-1], refs[-1]
    for index, source in enumerate(LATE):
        columns_out(
            place_ref, source, outs[index::len(LATE)], same_ref, cross_ref, gather_ref,
            spectral_ref, packed_ref,
        )


def led_kernel(
    place_ref, leds_ref, early_ref, window0_ref, window1_ref, window2_ref, window3_ref, measured_ref,
    same_ref, cross_ref, rows_ref, spread_ref, gather_ref, down_ref, across_ref,
    update0_ref, update1_ref, update2_ref, update3_ref, spectral_ref, stacked_ref, packed_ref,
):
    steps = stacked_ref.shape[0]
    half_size = stacked_ref.shape[4]
    stacked_ref[...] = early_ref[...]
    windows = (window0_ref, window2_ref), (window1_ref, window3_ref)
    for source, pair in zip(LATE, windows):
        columns_in(place_ref, source, pair, same_ref, cross_ref, spread_ref, packed_ref, stacked_ref)

    turn_re = jnp.concatenate([down_ref[0]] * (half_size // LANES), axis=1)
    turn_im = jnp.concatenate([down_ref[1]] * (half_size // LANES), axis=1)
    down, across = (turn_re, turn_im), (across_ref[0, 0:1], across_ref[1, 0:1])

    def turned(pair, by):
        return pair[0] * by[0] - pair[1] * by[1], pair[0] * by[1] + pair[1] * by[0]

    def plus(left, right):
        return left[0] + right[0], left[1] + right[1]

    def minus(left, right):
        return left[0] - right[0], left[1] - right[1]

    @pl.loop(0, steps)
    def _(step):
        led = leds_ref[step]

        def row_transform(half, parity):
            moved = table_dot(rows_ref[0], stacked_ref[step, parity, half])
            moved += table_dot(rows_ref[1], stacked_ref[step, parity, half])
            return moved[:half_size], moved[half_size:]

        def residual(field, row, lane):
            measured = measured_ref[led, pl.ds(row, half_size), pl.ds(lane, half_size)]
            real, imag = field
            factor = 1.0 - measured * lax.rsqrt(real * real + imag * imag + floor_sq)
            return real * factor, -imag * factor

        tops, lows = [], []
        for parity in range(2):
            first = row_transform(0, parity)
            second = turned(row_transform(1, parity), down)
            tops.append(plus(first, second))
            lows.append(minus(first, second))
        parts = []
        for row, (first, second) in ((0, tops), (half_size, lows)):
            second = turned(second, across)
            left = residual(plus(first, second), row, 0)
            right = residual(minus(first, second), row, half_size)
            parts.append((plus(left, right), turned(minus(left, right), across)))
        for parity in range(2):
            top, low = parts[0][parity], parts[1][parity]
            for half, value in enumerate((plus(top, low), turned(minus(top, low), down))):
                for part in range(2):
                    stacked_ref[step, parity, half, pl.ds(part * half_size, half_size)] = value[
                        part
                    ].astype(jnp.bfloat16)
        for parity in range(2):
            for half in range(2):
                moved = row_transform(half, parity)
                for part in range(2):
                    spectral_ref[
                        step, parity, pl.ds(half * half_size, half_size), pl.ds(part * half_size, half_size)
                    ] = moved[part].astype(jnp.bfloat16)

    updates = (update0_ref, update1_ref), (update2_ref, update3_ref)
    for source, pair in zip(EARLY, updates):
        columns_out(place_ref, source, pair, same_ref, cross_ref, gather_ref, spectral_ref, packed_ref)


def collect_kernel(peers, place_ref, starts_ref, *refs):
    updates = [refs[BACK_ORDER.index(peer)] for peer in range(8)]
    outs, total_ref = refs[8:-1], refs[-1]
    span = updates[0].shape[1]
    for peer, out_ref in zip(peers, outs):
        first = CORES * lax.rem(place_ref[NEAR] + peer, 4)
        for side in range(CORES):
            total_ref[...] = jnp.zeros_like(total_ref)
            for source in range(8):
                place = pl.ds(starts_ref[source, first + side], span)
                total_ref[place] = total_ref[place] + updates[source][first + side].astype(jnp.float32)
            out_ref[side] = total_ref[...].astype(out_ref.dtype)


def columns_kernel(place_ref, *refs):
    parts, outs = refs[:4], refs[4:]
    blocks = outs[0].shape[1]
    for peer in range(len(outs)):
        place = pl.ds(lax.rem(place_ref[COLUMN] + peer, len(outs)) * blocks, blocks)
        for side in range(CORES):
            total = parts[0][side, place].astype(jnp.float32)
            for part in parts[1:]:
                total = total + part[side, place].astype(jnp.float32)
            outs[peer][side] = total.astype(outs[peer].dtype)


def halves_kernel(place_ref, part0_ref, part1_ref, part2_ref, part3_ref, keep_ref, send_ref):
    core = place_ref[CORE]
    for out_ref, side in ((keep_ref, core), (send_ref, 1 - core)):
        total = part0_ref[side].astype(jnp.float32)
        for part_ref in (part1_ref, part2_ref, part3_ref):
            total = total + part_ref[side].astype(jnp.float32)
        out_ref[...] = total


def final_kernel(place_ref, own_ref, other_ref, spectrum_ref, out_ref, pair_ref):
    rows, width = spectrum_ref.shape[1:]
    low_half = low_lanes(rows // 2)
    first_core = place_ref[CORE] == 0
    back = lane_order(back=True)
    for group in range(width // LANES):
        for half in range(2):
            sums = []
            for block in (2 * group, 2 * group + 1):
                pair = (own_ref[block], other_ref[block])
                sums.append(jnp.where(first_core, pair[half], pair[1 - half]))
            real, imag = pack_pair(sums[0], sums[1], low_half)
            chosen = pl.ds(half, rows // 2, stride=2)
            pair_ref[group, 0, chosen] = -step_size * real
            pair_ref[group, 1, chosen] = step_size * imag
        lanes = pl.ds(group * LANES, LANES)
        for part in range(2):
            step = move_lanes(pair_ref[group, part], back)
            out_ref[part, :, lanes] = spectrum_ref[part, :, lanes] + step


def call(kernel, outs, inputs, mib, name, scalars=0, scratch=(), flops=0):
    size = sum(math.prod(out.shape) * out.dtype.itemsize for out in outs)
    size += sum(math.prod(array.shape) * array.dtype.itemsize for array in inputs)
    return pl.pallas_call(
        kernel,
        out_shape=tuple(outs),
        in_specs=[SMEM] * scalars + [VMEM] * (len(inputs) - scalars),
        out_specs=(VMEM,) * len(outs),
        scratch_shapes=list(scratch),
        compiler_params=params(mib),
        cost_estimate=pl.CostEstimate(flops=flops, bytes_accessed=size, transcendentals=0),
        name=name,
    )(*inputs)


TILES = DEPTHS * HEIGHTS * CORES


def tile_of(depth, height, core):
    return (depth % DEPTHS * HEIGHTS + height % HEIGHTS) * CORES + core


def tile_moves(even_move, odd_move):
    pairs = []
    for tile in range(TILES):
        depth, height, core = tile // (HEIGHTS * CORES), tile // CORES % HEIGHTS, tile % CORES
        pairs.append((tile, tile_of(*(odd_move if core else even_move)(depth, height))))
    return pairs


def far_moves(steps, side):
    return tile_moves(
        lambda depth, height: (depth + steps, height, side),
        lambda depth, height: (depth, height + steps, 1 - side),
    )


def near_moves(steps):
    return tile_moves(
        lambda depth, height: (depth, height + steps, 0),
        lambda depth, height: (depth + steps, height, 1),
    )


def reverse(moves):
    return [(target, source) for source, target in moves]


def send(array, moves, axis="tile"):
    return lax.ppermute(array, axis, moves)


def on_device(spectrum, pupil_field, amplitude, offsets):
    columns = lax.axis_size("col")
    tile, column = lax.axis_index("tile"), lax.axis_index("col")
    depth, height, core = tile // (HEIGHTS * CORES), tile // CORES % HEIGHTS, tile % CORES
    block_rows, own_width = spectrum.shape[1:]
    size = pupil_field.shape[1]
    span = size // block_rows
    own_blocks = own_width // block_rows
    band_blocks = own_blocks * columns
    rows = block_rows // 2
    bf16, f32 = jnp.bfloat16, jnp.float32
    shaped = lambda *shape, dtype=bf16: jax.ShapeDtypeStruct(shape, dtype)
    near = jnp.where(core == 0, height, depth)
    place = jnp.stack([depth, height, core, column, near]).astype(jnp.int32)
    swap = [(t, t ^ 1) for t in range(TILES)]

    wanted = jnp.arange(DEPTHS, dtype=jnp.int32) * span
    mine = offsets[None, :, 0] == wanted[:, None]
    slots = jnp.arange(offsets.shape[0], dtype=jnp.int32)[None]
    leds = jnp.roll(jnp.sum(jnp.where(mine, slots, 0), axis=1), -depth).astype(jnp.int32)
    firsts = jnp.sum(jnp.where(mine, offsets[None, :, 1], 0), axis=1).astype(jnp.int32)
    chip = jnp.stack([firsts, send(firsts, swap)])
    chips = jnp.stack([chip] + [send(chip, reverse(far_moves(steps, 0))) for steps in range(1, 4)])
    by_row = jnp.repeat(chips, CORES, axis=2)
    same_band = jnp.broadcast_to(lax.dynamic_slice_in_dim(chips, depth, 1, 2), by_row.shape)
    starts = jnp.where(core == 0, same_band, by_row).reshape(8, span).astype(jnp.int32)

    pairs = lambda width: [pltpu.VMEM((width // LANES, 2, block_rows, LANES), f32)]
    part_shape = (own_blocks, rows, LANES)
    tables = [jnp.asarray(table) for table in dft_tables(size, block_rows)]
    keep, give = call(
        prep_kernel,
        [shaped(*part_shape)] * 2,
        [place, spectrum],
        4,
        "prep",
        scalars=1,
        scratch=pairs(own_width),
    )
    joined, = call(
        join_kernel, [shaped(CORES, *part_shape)], [place, keep, send(give, swap)], 2, "join", scalars=1
    )
    along = lambda steps: [(c, (c + steps) % columns) for c in range(columns)]
    band, = call(
        band_kernel,
        [shaped(columns, CORES, *part_shape)],
        [place, joined] + [send(joined, along(steps), "col") for steps in range(1, columns)],
        4,
        "band",
        scalars=1,
    )
    near_parts = [band] + [send(band, near_moves(steps)) for steps in range(1, 4)]
    windows = call(
        select_kernel,
        [shaped(span, span, rows, LANES)] * 8,
        [place, starts] + near_parts,
        56,
        "select",
        scalars=2,
        scratch=[pltpu.VMEM((span, band_blocks, rows, LANES), bf16)],
    )
    far = [far_moves(steps, side) for steps in range(4) for side in range(CORES)]
    early = [2 * source + side for source in EARLY for side in range(CORES)]
    late = [2 * source + side for side in range(CORES) for source in LATE]
    incoming = [send(windows[peer], far[peer]) if peer else windows[0] for peer in early]
    late_windows = [send(windows[peer], far[peer]) for peer in late]

    pupil_field, incoming[1] = lax.optimization_barrier((pupil_field, incoming[1]))
    pupil_shape = shaped(2, span, span, rows, LANES, dtype=f32)
    same, cross = call(pupil_kernel, [pupil_shape] * 2, [pupil_field], 8, "pupil", scratch=[
        pltpu.VMEM((size // LANES, 2, size, LANES), f32)
    ])
    stacked_shape = (DEPTHS, 2, 2, size, size // 2)
    packed_scratch = pltpu.VMEM((2, size, size), bf16)
    window_shape = shaped(span, span, rows, LANES)
    rows_table, spread, gather, down, across = tables
    stacked, = call(
        first_kernel,
        [shaped(*stacked_shape)],
        [place, *incoming, same, cross, spread],
        12,
        "first",
        scalars=1,
        scratch=[packed_scratch],
        flops=48 * size**3,
    )
    *first_updates, spectral = call(
        led_kernel,
        [window_shape] * len(early) + [shaped(DEPTHS, 2, size, size)],
        [place, leds, stacked, *late_windows]
        + [amplitude, same, cross, rows_table, spread, gather, down, across],
        16,
        "leds",
        scalars=2,
        scratch=[pltpu.VMEM(stacked_shape, bf16), packed_scratch],
        flops=128 * size**3,
    )
    rest = call(
        last_kernel,
        [window_shape] * len(late),
        [place, spectral, same, cross, gather],
        12,
        "last",
        scalars=1,
        scratch=[packed_scratch],
        flops=48 * size**3,
    )
    returned = [None] * 8
    for peer, update in zip(early, first_updates):
        returned[peer] = send(update, reverse(far[peer])) if peer else update
    rest, returned[1] = lax.optimization_barrier((list(rest), returned[1]))
    for peer, update in zip(late, rest):
        returned[peer] = send(update, reverse(far[peer]))

    sum_shape = (CORES, band_blocks, rows, LANES)
    def collect(peers, kept_as):
        return call(
            functools.partial(collect_kernel, peers),
            [shaped(*sum_shape, dtype=kept_as)] * len(peers),
            [place, starts] + [returned[peer] for peer in BACK_ORDER],
            4,
            "collect",
            scalars=2,
            scratch=[pltpu.VMEM(sum_shape[1:], f32)],
        )

    sums = [None, *collect((1, 2, 3), bf16)]
    sums[0], = collect((0,), f32)
    near_sums = [sums[0]] + [send(sums[steps], near_moves(steps)) for steps in range(1, 4)]
    cut = call(
        columns_kernel,
        [shaped(CORES, *part_shape, dtype=f32)] + [shaped(CORES, *part_shape)] * (columns - 1),
        [place] + near_sums,
        4,
        "columns",
        scalars=1,
    )
    parts = [cut[0]] + [send(cut[steps], along(steps), "col") for steps in range(1, columns)]
    keep, give = call(
        halves_kernel, [shaped(*part_shape, dtype=f32)] * 2, [place] + parts, 2, "halves", scalars=1
    )
    return call(
        final_kernel,
        [shaped(*spectrum.shape, dtype=f32)],
        [place, keep, send(give, swap), spectrum],
        4,
        "final",
        scalars=1,
        scratch=pairs(own_width),
    )[0]


def solution(mesh):
    in_specs = (
        P(None, "tile", "col"),
        P(),
        P(("tile", "col"), None, None),
        P(("tile", "col"), None),
    )
    return jax.shard_map(
        on_device, mesh=mesh, in_specs=in_specs, out_specs=P(None, "tile", "col"), check_vma=False
    )
```
